32 devices in a mesh: dp: 2 (over x), seq: 16 (over z, y, core).
Axes of the slice: x: 2, y: 2, z: 4, core: 2. Of those that a mesh axis runs over, the one named last changes fastest.
Arguments:
- clean: bfloat16 [2, 4096, 768], P('dp', 'seq'), may hold values from -12 to 12
- out_cot: bfloat16 [2, 4096, 768], P('dp', 'seq'), may hold values from -6 to 6
- mask_bits: int32 [2, 256], P('dp', 'seq'), may hold values from 0 to 65535
- levels: int32 [2, 256], P('dp', 'seq'), may hold values from 1 to 16
- importance: int32 [2, 256, 2], P('dp', 'seq'), may hold values from 1 to 8
- w_query: bfloat16 [768, 768], replicated, may hold values from -0.21875 to 0.21875
- w_key: bfloat16 [768, 768], replicated, may hold values from -0.21875 to 0.21875
- w_value: bfloat16 [768, 768], replicated, may hold values from -0.21875 to 0.21875
- mask_embed: bfloat16 [768], replicated, may hold values from -6 to 6
Outputs:
- attn_out: bfloat16 [2, 4096, 768], P('dp', 'seq')
- clean_grad: float32 [2, 4096, 768], P('dp', 'seq')
The draws below stay inside these ranges and needn't reach their ends.
All inputs are finite; a program needn't handle non-finite values.
Results may differ from the reference program's by a relative error of at most 0.025.
Values may be sent and summed in bfloat16 or wider, within the bound.
No kernel may reach another device: no remote copies, remote signals or barrier semaphores. Data moves between devices by JAX's collectives and lax.ppermute only.
A program may use at most 64 MiB of HBM per device.

```python
import math
import jax
import jax.numpy as jnp
from jax import lax

HEADS = 12
HEAD_DIM = 64
D = 768
BLOCK = 16
WINDOW = 1024
TOK_DEV = 256
LEVELS = 16
IMP_MAX = 8
SEQLEN = 4096
NBLOCKS = 256
BATCH = 2


def draw_clean(key, part):
    return jnp.clip(jax.random.normal(key, (BATCH, SEQLEN, D), jnp.float32), -4.0, 4.0).astype(jnp.bfloat16)


def set_ends(drawn, own_key, smallest, high):
    extent = drawn.shape
    spot = [jax.random.randint(jax.random.fold_in(own_key, axis), (), 0, extent[axis]) for axis in range(len(extent))]
    drawn = drawn.at[tuple(spot)].set(smallest)
    longest = extent.index(max(extent))
    spot[longest] = (spot[longest] + 1) % extent[longest]
    return drawn.at[tuple(spot)].set(high)


def steps_of(key, dims, pieces, low, largest):
    def one(dim, shards_of):
        steps = jax.random.uniform(jax.random.fold_in(jax.random.fold_in(key, 6), dim), (shards_of,), jnp.float32, low / len(pieces), largest / len(pieces))
        return jnp.repeat(jnp.exp(steps), dims[dim] // shards_of).reshape((-1,) + (1,) * (len(dims) - dim - 1))

    gain = one(*pieces[0])
    for cut in pieces[1:]:
        gain = gain * one(*cut)
    return gain


def scatter_about(own_key, shape, scale, most, cuts=(), held_as=jnp.bfloat16):
    gain = steps_of(own_key, shape, cuts, -0.22, 0.18) if cuts else 1.0
    array = jax.random.normal(own_key, shape, jnp.float32) * scale * gain
    return jnp.minimum(jnp.maximum(array, -most), most).astype(held_as)


def setup_inputs(seed: int = 0) -> dict:
    splits = jax.random.split(jax.random.key(seed), 10)
    clean = draw_clean(jax.random.fold_in(splits[9], 71), 0)
    out_cot = scatter_about(splits[1], (BATCH, SEQLEN, D), 1.0, 6.0, ((0, 2), (1, 16)))
    mask_bits = set_ends(jax.random.randint(splits[2], (BATCH, NBLOCKS), 0, 65536), jax.random.fold_in(splits[2], 1), 0, 65535).astype(jnp.int32)
    levels = set_ends(jax.random.randint(splits[3], (BATCH, NBLOCKS), 1, LEVELS + 1), jax.random.fold_in(splits[3], 1), 1, LEVELS).astype(jnp.int32)
    importance = set_ends(jax.random.randint(splits[4], (BATCH, NBLOCKS, 2), 1, IMP_MAX + 1), jax.random.fold_in(splits[4], 1), 1, IMP_MAX).astype(jnp.int32)
    w_query = scatter_about(splits[5], (D, D), D ** -0.5, 0.21875)
    w_key = scatter_about(splits[6], (D, D), D ** -0.5, 0.21875)
    w_value = scatter_about(splits[7], (D, D), D ** -0.5, 0.21875)
    mask_embed = scatter_about(splits[8], (D,), 1.0, 6.0)
    return {"clean": clean, "out_cot": out_cot, "mask_bits": mask_bits, "levels": levels, "importance": importance, "w_query": w_query, "w_key": w_key, "w_value": w_value, "mask_embed": mask_embed}


EPS = 1e-06
CLIP = 0.25

def heads_of(rows):
    return rows.reshape(rows.shape[0], HEADS, HEAD_DIM).astype(jnp.float32)

def one_sequence(items, w_query, w_key, w_value, mask_embed):
    clean, cotangent, bits_row, level_row, ratio_row = items
    length = clean.shape[0]
    width = clean.shape[1]
    scale = 1.0 / math.sqrt(HEAD_DIM)
    place = jnp.arange(length, dtype=jnp.int32)
    block = place // BLOCK
    within = place % BLOCK
    bits = jnp.right_shift(bits_row[block], within) & 1
    masked = bits == 1
    noisy = jnp.where(masked[:, None], mask_embed[None, :], clean)
    key_clean = jnp.dot(clean, w_key, preferred_element_type=jnp.float32).astype(jnp.bfloat16)
    value_clean = jnp.dot(clean, w_value, preferred_element_type=jnp.float32).astype(jnp.bfloat16)
    query = jnp.dot(noisy, w_query, preferred_element_type=jnp.float32).astype(jnp.bfloat16)
    key_noisy = jnp.dot(noisy, w_key, preferred_element_type=jnp.float32).astype(jnp.bfloat16)
    value_noisy = jnp.dot(noisy, w_value, preferred_element_type=jnp.float32).astype(jnp.bfloat16)
    level_f = level_row.astype(jnp.float32)
    ratio_f = ratio_row.astype(jnp.float32)
    block_weight = LEVELS / level_f * (ratio_f[:, 0] / ratio_f[:, 1])
    token_weight = block_weight[block] * bits.astype(jnp.float32)
    grad_out = (cotangent.astype(jnp.float32) * token_weight[:, None]).astype(jnp.bfloat16)
    front = jnp.zeros((WINDOW, width), jnp.bfloat16)
    key_pad = jnp.concatenate([front, key_clean], axis=0)
    value_pad = jnp.concatenate([front, value_clean], axis=0)
    slab = WINDOW + TOK_DEV
    offsets = jnp.arange(slab, dtype=jnp.int32) - WINDOW
    local = jnp.arange(TOK_DEV, dtype=jnp.int32)
    local_block = local // BLOCK
    allow_noisy = local_block[None, :] == local_block[:, None]

    def tile(carry, index):
        key_grad, value_grad = carry
        start = (index * TOK_DEV).astype(jnp.int32)
        query_heads = heads_of(lax.dynamic_slice_in_dim(query, start, TOK_DEV, 0))
        nkey_heads = heads_of(lax.dynamic_slice_in_dim(key_noisy, start, TOK_DEV, 0))
        nvalue_heads = heads_of(lax.dynamic_slice_in_dim(value_noisy, start, TOK_DEV, 0))
        grad_rows = lax.dynamic_slice_in_dim(grad_out, start, TOK_DEV, 0)
        grad_heads = heads_of(grad_rows)
        key_heads = heads_of(lax.dynamic_slice_in_dim(key_pad, start, slab, 0))
        value_heads = heads_of(lax.dynamic_slice_in_dim(value_pad, start, slab, 0))
        key_pos = start + offsets
        q_start = (start + local) // BLOCK * BLOCK
        allow_clean = (key_pos[None, :] < q_start[:, None]) & (key_pos[None, :] >= q_start[:, None] - WINDOW) & (key_pos[None, :] >= 0)
        score_clean = jnp.einsum('qhe,khe->hqk', query_heads, key_heads) * scale
        score_noisy = jnp.einsum('qhe,khe->hqk', query_heads, nkey_heads) * scale
        score_clean = jnp.where(allow_clean[None], score_clean, -jnp.inf)
        score_noisy = jnp.where(allow_noisy[None], score_noisy, -jnp.inf)
        peak = jnp.maximum(lax.optimization_barrier(jnp.max(score_clean, axis=-1)), lax.optimization_barrier(jnp.max(score_noisy, axis=-1)))
        exp_clean = jnp.where(allow_clean[None], jnp.exp(score_clean - peak[..., None]), 0.0)
        exp_noisy = jnp.where(allow_noisy[None], jnp.exp(score_noisy - peak[..., None]), 0.0)
        denom = lax.optimization_barrier(jnp.sum(exp_clean, axis=-1)) + lax.optimization_barrier(jnp.sum(exp_noisy, axis=-1))
        prob_clean = exp_clean / denom[..., None]
        prob_noisy = exp_noisy / denom[..., None]
        weight_clean = prob_clean.astype(jnp.bfloat16).astype(jnp.float32)
        weight_noisy = prob_noisy.astype(jnp.bfloat16).astype(jnp.float32)
        mixed = jnp.einsum('hqk,khe->qhe', weight_clean, value_heads)
        mixed = mixed + jnp.einsum('hqk,khe->qhe', weight_noisy, nvalue_heads)
        attn_tile = mixed.reshape(TOK_DEV, width).astype(jnp.bfloat16)
        delta = lax.optimization_barrier(jnp.sum((grad_rows.astype(jnp.float32) * attn_tile.astype(jnp.float32)).reshape(TOK_DEV, HEADS, HEAD_DIM), axis=-1))
        dprob = jnp.einsum('qhe,khe->hqk', grad_heads, value_heads)
        dscore = (prob_clean * (dprob - delta.T[:, :, None]) * scale).astype(jnp.bfloat16).astype(jnp.float32)
        dkey = jnp.einsum('hqk,qhe->khe', dscore, query_heads).reshape(slab, width)
        dvalue = jnp.einsum('hqk,qhe->khe', weight_clean, grad_heads).reshape(slab, width)
        old_key = lax.dynamic_slice_in_dim(key_grad, start, slab, 0)
        old_value = lax.dynamic_slice_in_dim(value_grad, start, slab, 0)
        key_grad = lax.dynamic_update_slice_in_dim(key_grad, old_key + dkey, start, 0)
        value_grad = lax.dynamic_update_slice_in_dim(value_grad, old_value + dvalue, start, 0)
        return ((key_grad, value_grad), attn_tile)
    zeros = jnp.zeros((WINDOW + length, width), jnp.float32)
    tiles = jnp.arange(length // TOK_DEV, dtype=jnp.int32)
    (key_grad, value_grad), attn_tiles = lax.scan(tile, (zeros, zeros), tiles)
    attn_rows = attn_tiles.reshape(length, width)
    raw = jnp.dot(key_grad[WINDOW:], w_key.astype(jnp.float32).T, precision=lax.Precision.HIGHEST)
    raw = raw + jnp.dot(value_grad[WINDOW:], w_value.astype(jnp.float32).T, precision=lax.Precision.HIGHEST)
    return (attn_rows, raw)

def reference(clean, out_cot, mask_bits, levels, importance, w_query, w_key, w_value, mask_embed):

    def per_sequence(items):
        return one_sequence(items, w_query, w_key, w_value, mask_embed)
    attn_out, raw = lax.map(per_sequence, (clean, out_cot, mask_bits, levels, importance))
    rms = jnp.sqrt(jnp.mean(raw * raw) + EPS)
    factor = jnp.minimum(1.0, CLIP / rms)
    return (attn_out, raw * factor)
```

```python
import math

import jax
import jax.numpy as jnp
from jax import lax
from jax.experimental import pallas as pl
from jax.experimental.pallas import tpu as pltpu
from jax.sharding import PartitionSpec as P

HEADS = 12
HEAD_DIM = 64
BLOCK = 16
WINDOW = 1024
LEVELS = 16
EPS = 1e-06
CLIP = 0.25
LANES = 128
GROUP = 4
F32 = jnp.float32
BF16 = jnp.bfloat16
VMEM_LIMIT = 56 * 1024 * 1024
SCALE = 1.0 / math.sqrt(HEAD_DIM)


def iota(shape, dim):
    return lax.broadcasted_iota(jnp.int32, shape, dim)


def dot(a, b, precision=None):
    return jnp.dot(a, b, preferred_element_type=F32, precision=precision)


def dot_t(a, b, precision=None):
    return lax.dot_general(
        a, b, (((1,), (1,)), ((), ())), preferred_element_type=F32, precision=precision
    )


def token_mask_col(bits_row, tok):
    blocks = bits_row.shape[1]
    row, lane = iota((tok, blocks), 0), iota((tok, blocks), 1)
    bit = jnp.right_shift(jnp.broadcast_to(bits_row, (tok, blocks)), row % BLOCK) & 1
    return jnp.sum(jnp.where(row // BLOCK == lane, bit, 0).astype(F32), axis=1, keepdims=True)


def token_mask_row(bits_row, tok):
    blocks = bits_row.shape[1]
    diag = iota((blocks, blocks), 0) == iota((blocks, blocks), 1)
    col = jnp.sum(
        jnp.where(diag, jnp.broadcast_to(bits_row, (blocks, blocks)), 0).astype(F32),
        axis=1,
        keepdims=True,
    ).astype(jnp.int32)
    row, lane = iota((blocks, tok), 0), iota((blocks, tok), 1)
    bit = jnp.right_shift(jnp.broadcast_to(col, (blocks, tok)), lane % BLOCK) & 1
    return jnp.sum(jnp.where(lane // BLOCK == row, bit, 0).astype(F32), axis=0, keepdims=True)


def local_kernel(
    clean_ref, cot_ref, bits_ref, lev_ref, imp_ref, wq_ref, wk_ref, wv_ref, me_ref,
    q_ref, k_ref, v_ref, km_ref, vm_ref, a_ref, qk_ref, stats_ref,
):
    tok, width = clean_ref.shape
    blocks = tok // BLOCK
    bits = bits_ref[...]
    masked = token_mask_col(bits, tok)
    is_masked = masked > 0.5
    imp = imp_ref[...].astype(F32)
    ratio_col = imp[:, 0:1] / imp[:, 1:2]
    diag = iota((blocks, blocks), 0) == iota((blocks, blocks), 1)
    ratio = jnp.sum(
        jnp.where(diag, jnp.broadcast_to(ratio_col, (blocks, blocks)), 0.0), axis=0, keepdims=True
    )
    weight = LEVELS / lev_ref[...].astype(F32) * ratio
    row, lane = iota((tok, blocks), 0), iota((tok, blocks), 1)
    token_weight = masked * jnp.sum(
        jnp.where(row // BLOCK == lane, jnp.broadcast_to(weight, (tok, blocks)), 0.0),
        axis=1,
        keepdims=True,
    )
    grad = (cot_ref[...].astype(F32) * token_weight).astype(BF16)
    mask_rows = jnp.broadcast_to(me_ref[...], (BLOCK, width))
    rows = jnp.concatenate([clean_ref[...], mask_rows], axis=0)
    keys = dot(rows, wk_ref[...]).astype(BF16)
    values = dot(rows, wv_ref[...]).astype(BF16)
    queries = (dot(rows, wq_ref[...]).astype(BF16).astype(F32) * SCALE).astype(BF16)
    key, value = keys[:tok], values[:tok]
    qm, vm = queries[tok : tok + 1], values[tok : tok + 1]
    k_ref[...] = key
    v_ref[...] = value
    q_ref[...] = jnp.where(is_masked, qm.astype(F32), queries[:tok].astype(F32)).astype(BF16)
    km_ref[...] = keys[tok:]
    vm_ref[...] = values[tok:]
    head_of = iota((LANES, width), 1) // HEAD_DIM == iota((LANES, width), 0)
    spread = jnp.where(head_of, 1.0, 0.0).astype(BF16)
    qm_heads = jnp.where(head_of, jnp.broadcast_to(qm.astype(F32), (LANES, width)), 0.0).astype(BF16)
    score = dot_t(keys, qm_heads)
    own, mask_score = score[:tok], score[tok : tok + 1]
    a_ref[...] = own
    qk_ref[...] = dot_t(qm_heads, wk_ref[...])

    def block_sums(scores, vals):
        by_block = scores.reshape(blocks, BLOCK, LANES)
        top = jnp.max(by_block, axis=1)
        expo = jnp.exp(by_block - top[:, None, :])
        total = jnp.sum(expo, axis=1)
        wide = dot(expo.reshape(tok, LANES).astype(BF16), spread)
        mixed = jnp.sum((wide * vals).reshape(blocks, BLOCK, width), axis=1)
        return top, total, mixed

    value_f = value.astype(F32)
    top, total, mixed = block_sums(own, value_f)
    top_n, total_n, mixed_n = block_sums(
        jnp.where(is_masked, mask_score, own), jnp.where(is_masked, vm.astype(F32), value_f)
    )
    grad_sum = jnp.sum(grad.astype(F32).reshape(blocks, BLOCK, width), axis=1)
    grad_mix = dot_t(grad_sum * mixed_n, jnp.where(head_of, 1.0, 0.0), lax.Precision.HIGHEST)
    in_heads = iota((blocks, LANES), 1) < HEADS
    packed = jnp.where(in_heads, top, 0.0)
    for place, part in enumerate((total, top_n, total_n, grad_mix)):
        packed = packed + pltpu.roll(jnp.where(in_heads, part, 0.0), 16 * (place + 1), 1)
    high = packed.astype(BF16)
    rest = packed - high.astype(F32)
    mid = rest.astype(BF16)
    low = (rest - mid.astype(F32)).astype(BF16)
    stats_ref[0] = grad_sum.astype(BF16)
    stats_ref[1] = mixed.astype(BF16)
    stats_ref[2] = jnp.zeros((blocks, width), BF16)
    stats_ref[2, :, 0:LANES] = high
    stats_ref[2, :, LANES : 2 * LANES] = mid
    stats_ref[2, :, 2 * LANES : 3 * LANES] = low


def grad_kernel(
    place_ref, a_ref, v_ref, qk_ref, wv_ref, own_ref, back_ref, ahead_ref, y_ref, c_ref,
    raw_ref, square_ref, held,
):
    tok, width = v_ref.shape
    blocks = tok // BLOCK
    mine = place_ref[0]
    last = place_ref[1]
    at = mine % GROUP
    for part, ref in enumerate((back_ref, own_ref, ahead_ref)):
        held[part * GROUP + at] = ref[...]
        held[part * GROUP + (at ^ 2)] = y_ref[part]
        held[part * GROUP + (at ^ 1)] = c_ref[part]
        held[part * GROUP + (at ^ 3)] = c_ref[3 + part]
    near = GROUP * blocks
    count_b = 2 * near
    count_u = 3 * near
    pad_u = 4 * near
    grads = held[GROUP:, 0].reshape(count_b, width)
    mixed = held[:, 1].reshape(count_u, width)
    mixed = jnp.concatenate([mixed, jnp.zeros((pad_u - count_u, width), BF16)], axis=0)
    scalars = (
        held[:, 2, :, 0:LANES].astype(F32)
        + held[:, 2, :, LANES : 2 * LANES].astype(F32)
        + held[:, 2, :, 2 * LANES : 3 * LANES].astype(F32)
    ).reshape(count_u, LANES)
    flipped = jnp.concatenate([scalars, jnp.zeros((pad_u - count_u, LANES), F32)], axis=0).T
    of_b = scalars[near:]
    first_block = (mine - at - GROUP) * blocks
    b_at = iota((count_b, pad_u), 0) + near
    u_at = iota((count_b, pad_u), 1)
    seen = (u_at < b_at) & (u_at >= b_at - near) & (u_at + first_block >= 0)
    lane_b = iota((count_b, LANES), 1)
    peaks = jnp.zeros((count_b, LANES), F32)
    shares = jnp.zeros((count_b, LANES), F32)
    deltas = jnp.zeros((count_b, LANES), F32)
    for h in range(HEADS):
        pair = slice((h // 2) * LANES, (h // 2 + 1) * LANES)
        half = lane_b // HEAD_DIM == h % 2
        top = jnp.where(seen, flipped[h : h + 1], -jnp.inf)
        top_n = of_b[:, 32 + h : 33 + h]
        peak = jnp.maximum(jnp.max(top, axis=1, keepdims=True), top_n)
        expo = jnp.exp(top - peak)
        expo_n = jnp.exp(top_n - peak)
        den = jnp.sum(expo * flipped[16 + h : 17 + h], axis=1, keepdims=True)
        den = den + expo_n * of_b[:, 48 + h : 49 + h]
        out = dot(expo.astype(BF16), mixed[:, pair])
        delta = jnp.sum(jnp.where(half, out * grads[:, pair].astype(F32), 0.0), axis=1, keepdims=True)
        delta = (delta + expo_n * of_b[:, 64 + h : 65 + h]) / den
        peaks = jnp.where(lane_b == h, peak, peaks)
        shares = jnp.where(lane_b == h, 1.0 / den, shares)
        deltas = jnp.where(lane_b == h, delta, deltas)
    peaks, shares, deltas = peaks.T, shares.T, deltas.T
    own_at = near + at * blocks + iota((tok, count_b), 0) // BLOCK
    b_at = iota((tok, count_b), 1) + near
    seen = (own_at < b_at) & (own_at >= b_at - near) & (b_at + first_block < last)
    lane_u = iota((tok, LANES), 1)
    sigma = jnp.zeros((tok, LANES), F32)
    scores = a_ref[...]
    raw = jnp.zeros((tok, width), F32)
    for pair_at in range(HEADS // 2):
        pair = slice(pair_at * LANES, (pair_at + 1) * LANES)
        value = v_ref[:, pair]
        grad_pair = grads[:, pair]
        dvalue = None
        for h in (2 * pair_at, 2 * pair_at + 1):
            half = lane_u // HEAD_DIM == h % 2
            prob = jnp.exp(scores[:, h : h + 1] - peaks[h : h + 1]) * shares[h : h + 1]
            prob = jnp.where(seen, prob, 0.0)
            dprob = dot_t(jnp.where(half, value.astype(F32), 0.0).astype(BF16), grad_pair)
            term = jnp.sum(prob * (dprob - deltas[h : h + 1]), axis=1, keepdims=True)
            sigma = jnp.where(lane_u == h, term, sigma)
            part = dot(prob.astype(BF16), grad_pair)
            dvalue = part if dvalue is None else jnp.where(half, part, dvalue)
        high = dvalue.astype(BF16)
        low = (dvalue - high.astype(F32)).astype(BF16)
        raw = raw + dot_t(high, wv_ref[:, pair]) + dot_t(low, wv_ref[:, pair])
    raw = raw + dot(sigma, qk_ref[...], lax.Precision.HIGHEST)
    raw_ref[...] = raw
    square_ref[...] = jnp.full(square_ref.shape, jnp.sum(raw * raw), F32)


def attend_kernel(
    place_ref, bits_ref, q_ref, k_ref, v_ref, km_ref, vm_ref, wk_ref, wv_ref,
    far_ref, y_ref, c_ref, out_ref, keys, vals, score,
):
    tok, width = q_ref.shape
    mine = place_ref[0]
    bits = bits_ref[...]
    chunk_rows = (k_ref.shape[0],)
    for place, rows in enumerate((far_ref[...], y_ref[...], c_ref[0], c_ref[1])):
        keys[place] = dot(rows, wk_ref[...]).astype(BF16)
        vals[place] = dot(rows, wv_ref[...]).astype(BF16)
    row_b, col_b = iota((tok, tok), 0) // BLOCK, iota((tok, tok), 1) // BLOCK
    clear = token_mask_row(bits, tok) < 0.5
    own_bias = jnp.where((col_b < row_b) | ((col_b == row_b) & clear), 0.0, -jnp.inf)
    far_bias = jnp.where((col_b >= row_b) & (mine >= 4), 0.0, -jnp.inf)
    same = jnp.where(iota((tok, tok), 0) // BLOCK == iota((tok, tok), 1) // BLOCK, 1.0, 0.0)
    count = jnp.sum(same * token_mask_row(bits, tok), axis=1, keepdims=True)
    mask_bias = jnp.where(iota((tok, LANES), 1).astype(F32) < count, 0.0, -jnp.inf)
    biases = (far_bias,) + tuple(jnp.where(mine >= back, 0.0, -jnp.inf) for back in (2, 1, 3))
    lane = iota((tok, LANES), 1)

    def one_pair(pair_at, carry):
        pair = pl.ds(pl.multiple_of(pair_at * LANES, LANES), LANES)
        q_pair = q_ref[:, pair].astype(F32)
        k_own, v_own = k_ref[:, pair], v_ref[:, pair]
        k_mask = jnp.broadcast_to(km_ref[0:1, pair], (LANES, LANES))
        v_mask = jnp.broadcast_to(vm_ref[0:1, pair], (LANES, LANES))
        outs = []
        for half in range(2):
            here = lane // HEAD_DIM == half
            q_half = jnp.where(here, q_pair, 0.0).astype(BF16)
            s_own = dot_t(q_half, k_own) + own_bias
            s_mask = dot_t(q_half, k_mask) + mask_bias
            tops = [s_own[:, :LANES], s_own[:, LANES:], s_mask]
            for place in range(4):
                part = dot_t(q_half, keys[place, :, pair]) + biases[place]
                score[place] = part
                tops += [part[:, :LANES], part[:, LANES:]]
            while len(tops) > 1:
                tops = [jnp.maximum(*two) for two in zip(tops[::2], tops[1::2])] + (
                    [tops[-1]] if len(tops) % 2 else []
                )
            peak = jnp.max(tops[0], axis=1, keepdims=True)
            e_own, e_mask = jnp.exp(s_own - peak), jnp.exp(s_mask - peak)
            den = jnp.sum(e_own, axis=1, keepdims=True) + jnp.sum(e_mask, axis=1, keepdims=True)
            mixed = dot(e_own.astype(BF16), v_own) + dot(e_mask.astype(BF16), v_mask)
            for place in range(4):
                expo = jnp.exp(score[place] - peak)
                den = den + jnp.sum(expo, axis=1, keepdims=True)
                mixed = mixed + dot(expo.astype(BF16), vals[place, :, pair])
            outs.append(mixed / den)
        out_ref[:, pair] = jnp.where(lane < HEAD_DIM, outs[0], outs[1]).astype(BF16)
        return carry

    lax.fori_loop(0, HEADS // 2, one_pair, 0)


def scale_kernel(entries, square_ref, raw_ref, out_ref):
    total = jnp.sum(square_ref[:, 0:1], axis=0, keepdims=True)
    rms = jnp.sqrt(total / entries + EPS)
    out_ref[...] = raw_ref[...] * jnp.minimum(1.0, CLIP / rms)


def call(kernel, out_shape, scratch=(), smem=0, flops=0, **kw):
    def run(*args):
        spec = [pl.BlockSpec(memory_space=pltpu.SMEM)] * smem
        spec += [pl.BlockSpec(memory_space=pltpu.VMEM)] * (len(args) - smem)
        return pl.pallas_call(
            kernel,
            out_shape=out_shape,
            in_specs=spec,
            out_specs=jax.tree.map(lambda _: pl.BlockSpec(memory_space=pltpu.VMEM), out_shape),
            scratch_shapes=scratch,
            compiler_params=pltpu.CompilerParams(vmem_limit_bytes=VMEM_LIMIT),
            cost_estimate=pl.CostEstimate(flops=flops, bytes_accessed=4 << 20, transcendentals=0),
            **kw,
        )(*args)

    return run


def shift(rows, distance):
    devices = range(lax.axis_size("seq"))
    return lax.ppermute(rows, "seq", [(i, i + distance) for i in devices if i + distance in devices])


def swap(rows, bit):
    return lax.ppermute(rows, "seq", [(i, i ^ bit) for i in range(lax.axis_size("seq"))])


def on_device(clean, out_cot, mask_bits, levels, importance, w_query, w_key, w_value, mask_embed):
    clean_rows = clean[0]
    tok, width = clean_rows.shape
    blocks = tok // BLOCK
    place = lax.axis_index("seq")
    count = lax.axis_size("seq")
    where = jnp.stack([place, jnp.int32(count * blocks)]).astype(jnp.int32)

    def shape(*dims, dtype=BF16):
        return jax.ShapeDtypeStruct(dims, dtype)

    with jax.named_scope("halo"):
        far = shift(clean_rows, GROUP)
    with jax.named_scope("local"):
        q, k, v, km, vm, a, qk, stats = call(
            local_kernel,
            (
                shape(tok, width), shape(tok, width), shape(tok, width),
                shape(BLOCK, width), shape(BLOCK, width),
                shape(tok, LANES, dtype=F32), shape(LANES, width, dtype=F32),
                shape(3, blocks, width),
            ),
            flops=2_000_000_000,
        )(clean_rows, out_cot[0], mask_bits, levels, importance[0], w_query, w_key, w_value, mask_embed[None])
    with jax.named_scope("halo"):
        back, ahead = shift(stats, GROUP), shift(stats, -GROUP)
        mine3 = jnp.stack([back, stats, ahead])
        y3 = swap(mine3, 2)
        core6 = swap(jnp.concatenate([mine3, y3]), 1)
        two = swap(jnp.where(place & 2 == 0, clean_rows, far), 2)
        first = jnp.where(place & 1 == 0, clean_rows, two)
        second = jnp.where(place & 1 == 0, two, far)
        one_three = swap(jnp.stack([first, second]), 1)
    with jax.named_scope("grad"):
        parts = lax.axis_size("dp") * count
        raw, square = call(
            grad_kernel,
            (shape(tok, width, dtype=F32), shape(parts, LANES, dtype=F32)),
            scratch=[pltpu.VMEM((3 * GROUP, 3, blocks, width), BF16)],
            smem=1,
            flops=2_000_000_000,
        )(where, a, v, qk, w_value, stats, back, ahead, y3, core6)
        squares = lax.all_to_all(square, ("dp", "seq"), 0, 0)
    with jax.named_scope("attend"):
        attn = call(
            attend_kernel,
            shape(tok, width),
            scratch=[
                pltpu.VMEM((4, tok, width), BF16),
                pltpu.VMEM((4, tok, width), BF16),
                pltpu.VMEM((4, tok, tok), F32),
            ],
            smem=1,
            flops=8_000_000_000,
        )(where, mask_bits, q, k, v, km, vm, w_key, w_value, far, two, one_three)
    with jax.named_scope("clip"):
        entries = float(parts * tok * width)
        grad = call(lambda *refs: scale_kernel(entries, *refs), shape(tok, width, dtype=F32))(squares, raw)
    return attn[None], grad[None]


def solution(mesh):
    in_specs = (
        P("dp", "seq", None),
        P("dp", "seq", None),
        P("dp", "seq"),
        P("dp", "seq"),
        P("dp", "seq", None),
        P(),
        P(),
        P(),
        P(),
    )
    out_specs = (P("dp", "seq", None), P("dp", "seq", None))
    return jax.shard_map(
        on_device, mesh=mesh, in_specs=in_specs, out_specs=out_specs, check_vma=False
    )
```

```python
import math

import jax
import jax.numpy as jnp
from jax import lax
from jax.experimental import pallas as pl
from jax.experimental.pallas import tpu as pltpu
from jax.sharding import PartitionSpec as P

HEADS = 12
HEAD_DIM = 64
BLOCK = 16
WINDOW = 1024
LEVELS = 16
EPS = 1e-06
CLIP = 0.25
LANES = 128
NEVER = -1e30
GROUP = 4
F32 = jnp.float32
BF16 = jnp.bfloat16
VMEM_LIMIT = 56 * 1024 * 1024
SCALE = 1.0 / math.sqrt(HEAD_DIM)


def iota(shape, dim):
    return lax.broadcasted_iota(jnp.int32, shape, dim)


def dot(a, b, precision=None):
    return jnp.dot(a, b, preferred_element_type=F32, precision=precision)


def dot_t(a, b, precision=None):
    return lax.dot_general(
        a, b, (((1,), (1,)), ((), ())), preferred_element_type=F32, precision=precision
    )


def token_mask_col(bits_row, tok):
    blocks = bits_row.shape[1]
    row, lane = iota((tok, blocks), 0), iota((tok, blocks), 1)
    bit = jnp.right_shift(jnp.broadcast_to(bits_row, (tok, blocks)), row % BLOCK) & 1
    return jnp.sum(jnp.where(row // BLOCK == lane, bit, 0).astype(F32), axis=1, keepdims=True)


def token_mask_row(bits_row, tok):
    blocks = bits_row.shape[1]
    diag = iota((blocks, blocks), 0) == iota((blocks, blocks), 1)
    col = jnp.sum(
        jnp.where(diag, jnp.broadcast_to(bits_row, (blocks, blocks)), 0).astype(F32),
        axis=1,
        keepdims=True,
    ).astype(jnp.int32)
    row, lane = iota((blocks, tok), 0), iota((blocks, tok), 1)
    bit = jnp.right_shift(jnp.broadcast_to(col, (blocks, tok)), lane % BLOCK) & 1
    return jnp.sum(jnp.where(lane // BLOCK == row, bit, 0).astype(F32), axis=0, keepdims=True)


def start_all(copies):
    for copy in copies:
        copy.start()
    return copies


def columns(at, count):
    return slice(at * count, (at + 1) * count)


def both_heads(pair):
    low = iota(pair.shape, 1) < HEAD_DIM
    wide = pair.astype(F32)
    return jnp.concatenate([jnp.where(low, wide, 0.0), jnp.where(low, 0.0, wide)], axis=0).astype(BF16)


def local_kernel(
    clean_hbm, wk_hbm, wv_hbm, wq_hbm, cot_hbm, me_hbm, bits_hbm, lev_hbm, imp_hbm,
    stats_ref, a_ref, qk_ref, km_ref, vm_ref, q_hbm, k_hbm, v_hbm,
    clean_ref, wk_ref, wv_ref, wq_ref, cot_ref, me_ref, bits_ref, lev_ref, imp_ref,
    q_ref, k_ref, v_ref, in_sems, out_sems,
):
    sources = (clean_hbm, me_hbm, wk_hbm, wv_hbm, wq_hbm, bits_hbm, lev_hbm, imp_hbm, cot_hbm)
    targets = (clean_ref, me_ref, wk_ref, wv_ref, wq_ref, bits_ref, lev_ref, imp_ref, cot_ref)
    copies = start_all(
        [
            pltpu.make_async_copy(src, dst, in_sems.at[i])
            for i, (src, dst) in enumerate(zip(sources, targets))
        ]
    )
    tok, width = clean_ref.shape
    blocks = tok // BLOCK
    head_of = iota((LANES, width), 1) // HEAD_DIM == iota((LANES, width), 0)
    spread = jnp.where(head_of, 1.0, 0.0).astype(BF16)
    copies[0].wait()
    copies[1].wait()
    mask_rows = jnp.broadcast_to(me_ref[...].reshape(1, width), (BLOCK, width))
    rows = jnp.concatenate([clean_ref[...], mask_rows], axis=0)
    copies[2].wait()
    keys = dot(rows, wk_ref[...]).astype(BF16)
    k_ref[...] = keys[:tok]
    km_ref[...] = keys[tok:]
    copies[3].wait()
    values = dot(rows, wv_ref[...]).astype(BF16)
    v_ref[...] = values[:tok]
    vm_ref[...] = values[tok:]
    copies[4].wait()
    queries = (dot(rows, wq_ref[...]).astype(BF16).astype(F32) * SCALE).astype(BF16)
    for copy in copies[5:]:
        copy.wait()
    bits = bits_ref[...]
    masked = token_mask_col(bits, tok)
    is_masked = masked > 0.5
    qm, vm = queries[tok : tok + 1], values[tok : tok + 1]
    q_ref[...] = jnp.where(is_masked, qm.astype(F32), queries[:tok].astype(F32)).astype(BF16)
    outs = start_all(
        [
            pltpu.make_async_copy(src, dst, out_sems.at[i])
            for i, (src, dst) in enumerate(((q_ref, q_hbm), (k_ref, k_hbm), (v_ref, v_hbm)))
        ]
    )
    imp = imp_ref[...].astype(F32)
    weight = LEVELS / lev_ref[...].astype(F32) * (imp[0:1] / imp[1:2])
    row, lane = iota((tok, blocks), 0), iota((tok, blocks), 1)
    token_weight = masked * jnp.sum(
        jnp.where(row // BLOCK == lane, jnp.broadcast_to(weight, (tok, blocks)), 0.0),
        axis=1,
        keepdims=True,
    )
    grad = (cot_ref[...].astype(F32) * token_weight).astype(BF16)
    qm_heads = jnp.where(head_of, jnp.broadcast_to(qm.astype(F32), (LANES, width)), 0.0).astype(BF16)
    score = dot_t(keys, qm_heads)
    own, mask_score = score[:tok], score[tok : tok + 1]
    a_ref[...] = own
    back = dot_t(qm_heads, wk_ref[...])[:BLOCK]
    high = back.astype(BF16)
    low = (back - high.astype(F32)).astype(BF16)
    qk_ref[...] = jnp.zeros(qk_ref.shape, BF16)
    qk_ref[0:BLOCK] = high
    qk_ref[BLOCK : 2 * BLOCK] = high
    qk_ref[2 * BLOCK : 3 * BLOCK] = low

    def block_sums(scores, vals):
        by_block = scores.reshape(blocks, BLOCK, LANES)
        top = jnp.max(by_block, axis=1)
        expo = jnp.exp(by_block - top[:, None, :])
        total = jnp.sum(expo, axis=1)
        share = expo * (1.0 / total)[:, None, :]
        wide = dot(share.reshape(tok, LANES).astype(BF16), spread)
        mixed = jnp.sum((wide * vals).reshape(blocks, BLOCK, width), axis=1)
        return top + jnp.log(total), mixed

    value_f = values[:tok].astype(F32)
    top, mixed = block_sums(own, value_f)
    top_n, mixed_n = block_sums(
        jnp.where(is_masked, mask_score, own), jnp.where(is_masked, vm.astype(F32), value_f)
    )
    grad_sum = jnp.sum(grad.astype(F32).reshape(blocks, BLOCK, width), axis=1)
    product = grad_sum * mixed_n
    high = product.astype(BF16)
    low = (product - high.astype(F32)).astype(BF16)
    grad_mix = dot_t(high, spread) + dot_t(low, spread)
    in_heads = iota((blocks, LANES), 1) < HEADS
    packed = jnp.where(in_heads, top, 0.0)
    for place, part in enumerate((top_n, grad_mix)):
        packed = packed + pltpu.roll(jnp.where(in_heads, part, 0.0), 16 * (place + 1), 1)
    high = packed.astype(BF16)
    rest = packed - high.astype(F32)
    mid = rest.astype(BF16)
    low = (rest - mid.astype(F32)).astype(BF16)
    stats_ref[0] = grad_sum.astype(BF16)
    stats_ref[1] = mixed.astype(BF16)
    stats_ref[2] = jnp.zeros((blocks, width), BF16)
    stats_ref[2, :, 0:LANES] = high
    stats_ref[2, :, LANES : 2 * LANES] = mid
    stats_ref[2, :, 2 * LANES : 3 * LANES] = low
    for copy in outs:
        copy.wait()


def grad_kernel(
    place_ref, own_hbm, back_hbm, ahead_hbm, y_hbm, c_hbm, a_hbm, v_hbm, qk_hbm, wv_hbm,
    square_ref, raw_hbm,
    held, a_ref, v_ref, qk_ref, wv_ref, dvalues, raw_ref, in_sems, out_sems,
):
    tok, width = v_ref.shape
    blocks = tok // BLOCK
    mine = place_ref[0]
    last = place_ref[1]
    at = mine % GROUP
    held[...] = jnp.zeros(held.shape, BF16)
    y_side = jnp.where(at & 2 == 0, 0, 2 * GROUP)
    c_side = jnp.where(at & 1 == 0, 0, 2 * GROUP)
    moves = (
        (back_hbm, held.at[at]),
        (own_hbm, held.at[GROUP + at]),
        (ahead_hbm, held.at[2 * GROUP + at]),
        (y_hbm.at[0], held.at[GROUP + (at ^ 2)]),
        (y_hbm.at[1], held.at[y_side + (at ^ 2)]),
        (c_hbm.at[0], held.at[GROUP + (at ^ 1)]),
        (c_hbm.at[1], held.at[c_side + (at ^ 1)]),
        (c_hbm.at[2], held.at[GROUP + (at ^ 3)]),
        (c_hbm.at[3], held.at[y_side + (at ^ 3)]),
        (a_hbm, a_ref),
        (v_hbm, v_ref),
        (qk_hbm, qk_ref),
        (wv_hbm, wv_ref),
    )
    copies = start_all(
        [pltpu.make_async_copy(src, dst, in_sems.at[i]) for i, (src, dst) in enumerate(moves)]
    )
    near = GROUP * blocks
    count_b = 2 * near
    count_u = 3 * near
    pad_u = 4 * near
    first_block = (mine - at - GROUP) * blocks
    u_at = iota((count_u, count_b), 0)
    b_at = iota((count_u, count_b), 1) + near
    seen = (u_at < b_at) & (u_at >= b_at - near) & (u_at + first_block >= 0)
    bias = jnp.where(seen, 0.0, -jnp.inf)
    for copy in copies[:9]:
        copy.wait()
    grads = held[GROUP:, 0].reshape(count_b, width)
    mixed = held[:, 1].reshape(count_u, width)
    scalars = (
        held[:, 2, :, 0:LANES].astype(F32)
        + held[:, 2, :, LANES : 2 * LANES].astype(F32)
        + held[:, 2, :, 2 * LANES : 3 * LANES].astype(F32)
    ).reshape(count_u, LANES)
    padded = jnp.concatenate(
        [scalars[near:], jnp.zeros((pad_u - count_b, LANES), F32)], axis=0
    )
    flipped = padded.T[:, :count_b]
    logs, deltas = [], []
    for pair_at in range(HEADS // 2):
        pair = columns(pair_at, LANES)
        products = dot_t(both_heads(mixed[:, pair]), grads[:, pair])
        for half in range(2):
            h = 2 * pair_at + half
            top = scalars[:, h : h + 1] + bias
            top_n = flipped[16 + h : 17 + h]
            peak = jnp.maximum(jnp.max(top, axis=0, keepdims=True), top_n)
            expo = jnp.exp(top - peak)
            expo_n = jnp.exp(top_n - peak)
            den = jnp.sum(expo, axis=0, keepdims=True) + expo_n
            delta = jnp.sum(expo * products[columns(half, count_u)], axis=0, keepdims=True)
            delta = (delta + expo_n * flipped[32 + h : 33 + h]) / den
            logs.append(peak + jnp.log(den))
            deltas.append(delta)
    own_at = near + at * blocks + iota((tok, count_b), 0) // BLOCK
    b_at = iota((tok, count_b), 1) + near
    seen = (own_at < b_at) & (own_at >= b_at - near) & (b_at + first_block < last)
    bias = jnp.where(seen, 0.0, -jnp.inf)
    lane_u = iota((tok, LANES), 1)
    sigma = jnp.zeros((tok, LANES), F32)
    copies[9].wait()
    copies[10].wait()
    scores = a_ref[...]
    for pair_at in range(HEADS // 2):
        pair = columns(pair_at, LANES)
        grad_pair = grads[:, pair]
        dprobs = dot_t(both_heads(v_ref[:, pair]), grad_pair)
        probs = []
        for half in range(2):
            h = 2 * pair_at + half
            prob = jnp.exp(scores[:, h : h + 1] - logs[h] + bias)
            term = prob * (dprobs[columns(half, tok)] - deltas[h])
            sigma = jnp.where(lane_u == h, jnp.sum(term, axis=1, keepdims=True), sigma)
            probs.append(prob.astype(BF16))
        parts = dot(jnp.concatenate(probs, axis=0), grad_pair)
        dvalues[:, pair] = jnp.where(lane_u < HEAD_DIM, parts[:tok], parts[tok:]).astype(BF16)
    high = sigma.astype(BF16).astype(F32)
    low = (sigma - high).astype(BF16).astype(F32)
    split = (high + pltpu.roll(low, 16, 1) + pltpu.roll(high, 32, 1)).astype(BF16)
    copies[11].wait()
    copies[12].wait()
    squares = jnp.zeros((1, 1), F32)
    outs = []
    part = 2 * LANES
    for at_part in range(width // part):
        cols = columns(at_part, part)
        raw = dot_t(dvalues[...], wv_ref[cols]) + dot(split, qk_ref[:, cols])
        raw_ref[:, cols] = raw
        outs.append(
            pltpu.make_async_copy(raw_ref.at[:, cols], raw_hbm.at[:, cols], out_sems.at[at_part])
        )
        outs[-1].start()
        total = jnp.sum(raw * raw, axis=0, keepdims=True)
        squares = squares + jnp.sum(total, axis=1, keepdims=True)
    square_ref[...] = jnp.broadcast_to(squares, square_ref.shape)
    for copy in outs:
        copy.wait()


def own_kernel(
    q_hbm, k_hbm, v_hbm, km_ref, vm_ref, bits_ref,
    log_ref, mixed_ref,
    q_ref, k_ref, v_ref, in_sems,
):
    tok, width = q_ref.shape
    pairs = HEADS // 2
    copies = start_all(
        [
            pltpu.make_async_copy(src, dst, in_sems.at[i])
            for i, (src, dst) in enumerate(((q_hbm, q_ref), (k_hbm, k_ref), (v_hbm, v_ref)))
        ]
    )
    row_b, col_b = iota((tok, tok), 0) // BLOCK, iota((tok, tok), 1) // BLOCK
    masked = token_mask_row(bits_ref[...], tok)
    own_bias = jnp.where((col_b < row_b) | ((col_b == row_b) & (masked < 0.5)), 0.0, -jnp.inf)
    count = jnp.sum(jnp.where(row_b == col_b, masked, 0.0), axis=1, keepdims=True)
    mask_bias = jnp.where(iota((tok, LANES), 1).astype(F32) < count, 0.0, -jnp.inf)
    bias = jnp.concatenate([own_bias, mask_bias], axis=1)
    bias = jnp.concatenate([bias, bias], axis=0)
    lane = iota((tok, LANES), 1)
    logs = jnp.zeros((tok, LANES), F32)
    for copy in copies:
        copy.wait()
    for pair_at in range(pairs):
        pair = columns(pair_at, LANES)
        k_mask = jnp.broadcast_to(km_ref[0:1, pair], (LANES, LANES))
        v_mask = jnp.broadcast_to(vm_ref[0:1, pair], (LANES, LANES))
        keys = jnp.concatenate([k_ref[:, pair], k_mask], axis=0)
        vals = jnp.concatenate([v_ref[:, pair], v_mask], axis=0)
        score = dot_t(both_heads(q_ref[:, pair]), keys) + bias
        peak = jnp.max(score, axis=1, keepdims=True)
        expo = jnp.exp(score - peak)
        den = jnp.sum(expo, axis=1, keepdims=True)
        mixed = dot(expo.astype(BF16), vals) / den
        log = peak + jnp.log(den)
        logs = jnp.where(lane == 2 * pair_at, log[:tok], logs)
        logs = jnp.where(lane == 2 * pair_at + 1, log[tok:], logs)
        mixed_ref[:, pair] = jnp.where(lane < HEAD_DIM, mixed[:tok], mixed[tok:]).astype(BF16)
    log_ref[...] = logs


def rest_kernel(
    place_ref, far_hbm, two_hbm, ones_hbm,
    wk_hbm, wv_hbm, q_hbm, mixed_hbm, log_hbm, after_hbm,
    out_ref,
    rows, wk_ref, wv_ref, q_ref, mixed_ref, log_ref, keys, vals, total_ref, in_sems,
):
    tok, width = q_ref.shape
    shards = rows.shape[0]
    mine = place_ref[0]
    part = 2 * LANES
    parts = width // part

    def load(src, dst, at):
        return pltpu.make_async_copy(src, dst, in_sems.at[at])

    weights = []
    for at in range(parts):
        cols = columns(at, part)
        for i, (src, dst) in enumerate(((wk_hbm, wk_ref), (wv_hbm, wv_ref))):
            weights.append(load(src.at[:, cols], dst.at[:, cols], shards + 2 * at + i))
    others = [
        load(src, dst, shards + 2 * parts + i)
        for i, (src, dst) in enumerate(((q_hbm, q_ref), (mixed_hbm, mixed_ref), (log_hbm, log_ref)))
    ]
    shard_copies = [
        load(src, rows.at[at], at)
        for at, src in enumerate((far_hbm, two_hbm, ones_hbm.at[0], ones_hbm.at[1]))
    ]
    start_all(shard_copies[:1])
    start_all(weights[:2])
    start_all(shard_copies[1:])
    start_all(others)
    start_all(weights[2:])
    row_b, col_b = iota((tok, tok), 0) // BLOCK, iota((tok, tok), 1) // BLOCK
    far_bias = jnp.where((col_b >= row_b) & (mine >= GROUP), 0.0, NEVER)
    far_bias = jnp.concatenate([far_bias, far_bias], axis=0)
    biases = [far_bias] + [jnp.where(mine >= back, 0.0, NEVER) for back in (2, 1, 3)]
    lane = iota((tok, LANES), 1)
    for at in range(parts):
        cols = columns(at, part)
        for copy in weights[2 * at : 2 * at + 2]:
            copy.wait()
        for place in range(shards):
            if at == 0:
                shard_copies[place].wait()
            span = columns(place, tok)
            keys[span, cols] = dot(rows[place], wk_ref[:, cols]).astype(BF16)
            vals[span, cols] = dot(rows[place], wv_ref[:, cols]).astype(BF16)
    for copy in others:
        copy.wait()
    logs = jnp.zeros((tok, LANES), F32)
    for pair_at in range(HEADS // 2):
        pair = columns(pair_at, LANES)
        score = dot_t(both_heads(q_ref[:, pair]), keys[:, pair])
        pieces = [score[:, columns(place, tok)] + biases[place] for place in range(shards)]
        peak = jnp.maximum(jnp.maximum(pieces[0], pieces[1]), jnp.maximum(pieces[2], pieces[3]))
        peak = jnp.max(peak, axis=1, keepdims=True)
        pieces = [jnp.exp(piece - peak) for piece in pieces]
        den = jnp.sum((pieces[0] + pieces[1]) + (pieces[2] + pieces[3]), axis=1, keepdims=True)
        expo = jnp.concatenate([piece.astype(BF16) for piece in pieces], axis=1)
        mixed = dot(expo, vals[:, pair]) / den
        log = peak + jnp.log(den)
        logs = jnp.where(lane == 2 * pair_at, log[:tok], logs)
        logs = jnp.where(lane == 2 * pair_at + 1, log[tok:], logs)
        total_ref[:, pair] = jnp.where(lane < HEAD_DIM, mixed[:tok], mixed[tok:])
    share = 1.0 / (1.0 + jnp.exp(logs - log_ref[...]))
    high = share.astype(BF16)
    less = (share - high.astype(F32)).astype(BF16)
    head_of = iota((LANES, width), 1) // HEAD_DIM == iota((LANES, width), 0)
    spread = jnp.where(head_of, 1.0, 0.0).astype(BF16)
    share = dot(high, spread) + dot(less, spread)
    total = total_ref[...]
    out_ref[...] = (total + share * (mixed_ref[...].astype(F32) - total)).astype(BF16)


def scale_kernel(entries, square_hbm, raw_hbm, out_hbm, square_ref, raw_ref, in_sems, out_sems):
    tok = raw_ref.shape[0]
    pieces = 4
    spans = [columns(at, tok // pieces) for at in range(pieces)]
    first = pltpu.make_async_copy(square_hbm, square_ref, in_sems.at[pieces])
    first.start()
    copies = start_all(
        [
            pltpu.make_async_copy(raw_hbm.at[span], raw_ref.at[span], in_sems.at[at])
            for at, span in enumerate(spans)
        ]
    )
    first.wait()
    total = jnp.sum(square_ref[:, 0:1], axis=0, keepdims=True)
    rms = jnp.sqrt(total / entries + EPS)
    factor = jnp.minimum(1.0, CLIP / rms)
    outs = []
    for at, span in enumerate(spans):
        copies[at].wait()
        raw_ref[span] = raw_ref[span] * factor
        outs.append(pltpu.make_async_copy(raw_ref.at[span], out_hbm.at[span], out_sems.at[at]))
        outs[-1].start()
    for copy in outs:
        copy.wait()


def call(kernel, out_shape, hbm_out, args, scratch, smem=(), vmem=(), flops=0):
    args = [pltpu.with_memory_space_constraint(array, pltpu.HBM) for array in (*args, *vmem)]
    kinds = [pltpu.SMEM] * len(smem) + [pl.ANY] * (len(args) - len(vmem)) + [pltpu.VMEM] * len(vmem)
    out_kinds = [pltpu.VMEM] * (len(out_shape) - hbm_out) + [pl.ANY] * hbm_out
    return pl.pallas_call(
        kernel,
        out_shape=[pltpu.HBM(array.shape, array.dtype) for array in out_shape],
        in_specs=[pl.BlockSpec(memory_space=kind) for kind in kinds],
        out_specs=[pl.BlockSpec(memory_space=kind) for kind in out_kinds],
        scratch_shapes=scratch,
        compiler_params=pltpu.CompilerParams(vmem_limit_bytes=VMEM_LIMIT),
        cost_estimate=pl.CostEstimate(flops=flops, bytes_accessed=1 << 10, transcendentals=0),
    )(*smem, *args)


def shift(rows, distance):
    devices = range(lax.axis_size("seq"))
    return lax.ppermute(rows, "seq", [(i, i + distance) for i in devices if i + distance in devices])


def swap(rows, bit, test=None):
    devices = range(lax.axis_size("seq"))
    return lax.ppermute(rows, "seq", [(i, i ^ bit) for i in devices if test is None or test(i)])


def on_device(clean, out_cot, mask_bits, levels, importance, w_query, w_key, w_value, mask_embed):
    clean_rows = clean[0]
    tok, width = clean_rows.shape
    blocks = tok // BLOCK
    place = lax.axis_index("seq")
    count = lax.axis_size("seq")
    parts = lax.axis_size("dp") * count
    where = jnp.stack([place, jnp.int32(count * blocks)]).astype(jnp.int32)
    rows = (tok, width)
    square_w = (width, width)

    def like(*dims, dtype=BF16):
        return jax.ShapeDtypeStruct(dims, dtype)

    def vmem(*dims, dtype=BF16):
        return pltpu.VMEM(dims, dtype)

    def sems(count):
        return pltpu.SemaphoreType.DMA((count,))

    with jax.named_scope("local"):
        ratio = importance[0].T
        stats, a, qk, km, vm, q, k, v = call(
            local_kernel,
            [
                like(3, blocks, width), like(tok, LANES, dtype=F32), like(LANES, width),
                like(BLOCK, width), like(BLOCK, width), like(*rows), like(*rows), like(*rows),
            ],
            3,
            [clean_rows, w_key, w_value, w_query, out_cot[0], mask_embed, mask_bits, levels, ratio],
            [
                vmem(*rows), vmem(*square_w), vmem(*square_w), vmem(*square_w), vmem(*rows),
                vmem(width), vmem(1, blocks, dtype=jnp.int32), vmem(1, blocks, dtype=jnp.int32),
                vmem(2, blocks, dtype=jnp.int32), vmem(*rows), vmem(*rows), vmem(*rows),
                sems(9), sems(3),
            ],
            flops=1_000_000_000,
        )
    with jax.named_scope("halo"):
        back, ahead = shift(stats, GROUP), shift(stats, -GROUP)
        back, ahead, clean_rows = lax.optimization_barrier((back, ahead, clean_rows))
        y2 = swap(jnp.stack([stats, jnp.where(place & 2 == 0, ahead, back)]), 2)
        far = shift(clean_rows, GROUP)
    with jax.named_scope("own"):
        log, mixed = call(
            own_kernel,
            [like(tok, LANES, dtype=F32), like(*rows)],
            0,
            [q, k, v],
            [vmem(*rows), vmem(*rows), vmem(*rows), sems(3)],
            vmem=[km, vm, mask_bits],
            flops=4_000_000_000,
        )
    with jax.named_scope("halo"):
        y2, log, clean_rows = lax.optimization_barrier((y2, log, clean_rows))
        y_last = swap(clean_rows, 2, lambda i: i & 2 == 0)
        y_first = swap(far, 2, lambda i: i & 2 == 2)
        sides = jnp.stack([stats, jnp.where(place & 1 == 0, ahead, back)])
        core4 = swap(jnp.concatenate([sides, y2]), 1)
    with jax.named_scope("grad"):
        square, raw = call(
            grad_kernel,
            [like(parts, LANES, dtype=F32), like(*rows, dtype=F32)],
            1,
            [stats, back, ahead, y2, core4, a, v, qk, w_value],
            [
                vmem(3 * GROUP, 3, blocks, width), vmem(tok, LANES, dtype=F32), vmem(*rows),
                vmem(LANES, width), vmem(*square_w), vmem(*rows), vmem(*rows, dtype=F32),
                sems(13), sems(width // LANES // 2),
            ],
            smem=[where],
            flops=4_000_000_000,
        )
        y_first, y_last, square = lax.optimization_barrier((y_first, y_last, square))
        two = jnp.where(place & 2 == 0, y_first, y_last)
        mine = place & 1 == 0
        ones = swap(jnp.stack([jnp.where(mine, clean_rows, two), jnp.where(mine, two, far)]), 1)
        squares = lax.all_to_all(square, ("dp", "seq"), 0, 0)
    with jax.named_scope("rest"):
        (attn,) = call(
            rest_kernel,
            [like(*rows)],
            0,
            [far, two, ones, w_key, w_value, q, mixed, log, square],
            [
                vmem(GROUP, *rows), vmem(*square_w), vmem(*square_w), vmem(*rows), vmem(*rows),
                vmem(tok, LANES, dtype=F32), vmem(GROUP * tok, width), vmem(GROUP * tok, width),
                vmem(*rows, dtype=F32), sems(GROUP + width // LANES + 3),
            ],
            smem=[where],
            flops=8_000_000_000,
        )
    with jax.named_scope("clip"):
        squares, attn = lax.optimization_barrier((squares, attn))
        entries = float(parts * tok * width)
        (grad,) = call(
            lambda *refs: scale_kernel(entries, *refs),
            [like(*rows, dtype=F32)],
            1,
            [squares, raw],
            [vmem(parts, LANES, dtype=F32), vmem(*rows, dtype=F32), sems(5), sems(4)],
        )
    return attn[None], grad[None]


def solution(mesh):
    in_specs = (
        P("dp", "seq", None),
        P("dp", "seq", None),
        P("dp", "seq"),
        P("dp", "seq"),
        P("dp", "seq", None),
        P(),
        P(),
        P(),
        P(),
    )
    out_specs = (P("dp", "seq", None), P("dp", "seq", None))
    return jax.shard_map(
        on_device, mesh=mesh, in_specs=in_specs, out_specs=out_specs, check_vma=False
    )
```

```python
import math

import jax
import jax.numpy as jnp
from jax import lax
from jax.experimental import pallas as pl
from jax.experimental.pallas import tpu as pltpu
from jax.sharding import PartitionSpec as P

HEADS = 12
HEAD_DIM = 64
BLOCK = 16
WINDOW = 1024
LEVELS = 16
EPS = 1e-06
CLIP = 0.25
LANES = 128
NEVER = -1e30
GROUP = 4
F32 = jnp.float32
BF16 = jnp.bfloat16
VMEM_LIMIT = 32 * 1024 * 1024
SCALE = 1.0 / math.sqrt(HEAD_DIM)


def iota(shape, dim):
    return lax.broadcasted_iota(jnp.int32, shape, dim)


def dot(a, b, precision=None):
    return jnp.dot(a, b, preferred_element_type=F32, precision=precision)


def dot_t(a, b, precision=None):
    return lax.dot_general(
        a, b, (((1,), (1,)), ((), ())), preferred_element_type=F32, precision=precision
    )


def token_mask_col(bits_row, tok):
    blocks = bits_row.shape[1]
    row, lane = iota((tok, blocks), 0), iota((tok, blocks), 1)
    bit = jnp.right_shift(jnp.broadcast_to(bits_row, (tok, blocks)), row % BLOCK) & 1
    return jnp.sum(jnp.where(row // BLOCK == lane, bit, 0).astype(F32), axis=1, keepdims=True)


def token_mask_row(bits_row, tok):
    blocks = bits_row.shape[1]
    diag = iota((blocks, blocks), 0) == iota((blocks, blocks), 1)
    col = jnp.sum(
        jnp.where(diag, jnp.broadcast_to(bits_row, (blocks, blocks)), 0).astype(F32),
        axis=1,
        keepdims=True,
    ).astype(jnp.int32)
    row, lane = iota((blocks, tok), 0), iota((blocks, tok), 1)
    bit = jnp.right_shift(jnp.broadcast_to(col, (blocks, tok)), lane % BLOCK) & 1
    return jnp.sum(jnp.where(lane // BLOCK == row, bit, 0).astype(F32), axis=0, keepdims=True)


def start_all(copies):
    for copy in copies:
        copy.start()
    return copies


def columns(at, count):
    return slice(at * count, (at + 1) * count)


def both_heads(pair):
    low = iota(pair.shape, 1) < HEAD_DIM
    wide = pair.astype(F32)
    return jnp.concatenate([jnp.where(low, wide, 0.0), jnp.where(low, 0.0, wide)], axis=0).astype(BF16)


def local_kernel(
    clean_hbm, wk_hbm, wv_hbm, wq_hbm, cot_hbm, me_hbm, bits_hbm, lev_hbm, imp_hbm,
    stats_ref, a_ref, qk_ref, km_ref, vm_ref, q_hbm, k_hbm, v_hbm,
    clean_ref, wk_ref, wv_ref, wq_ref, cot_ref, me_ref, bits_ref, lev_ref, imp_ref,
    q_ref, k_ref, v_ref, in_sems, out_sems,
):
    sources = (clean_hbm, me_hbm, wk_hbm, wv_hbm, wq_hbm, bits_hbm, lev_hbm, imp_hbm, cot_hbm)
    targets = (clean_ref, me_ref, wk_ref, wv_ref, wq_ref, bits_ref, lev_ref, imp_ref, cot_ref)
    copies = start_all(
        [
            pltpu.make_async_copy(src, dst, in_sems.at[i])
            for i, (src, dst) in enumerate(zip(sources, targets))
        ]
    )
    tok, width = clean_ref.shape
    blocks = tok // BLOCK
    head_of = iota((LANES, width), 1) // HEAD_DIM == iota((LANES, width), 0)
    spread = jnp.where(head_of, 1.0, 0.0).astype(BF16)
    copies[0].wait()
    copies[1].wait()
    mask_rows = jnp.broadcast_to(me_ref[...].reshape(1, width), (BLOCK, width))
    rows = jnp.concatenate([clean_ref[...], mask_rows], axis=0)
    copies[2].wait()
    keys = dot(rows, wk_ref[...]).astype(BF16)
    k_ref[...] = keys[:tok]
    km_ref[...] = keys[tok:]
    copies[3].wait()
    values = dot(rows, wv_ref[...]).astype(BF16)
    v_ref[...] = values[:tok]
    vm_ref[...] = values[tok:]
    copies[4].wait()
    queries = (dot(rows, wq_ref[...]).astype(BF16).astype(F32) * SCALE).astype(BF16)
    for copy in copies[5:]:
        copy.wait()
    bits = bits_ref[...]
    masked = token_mask_col(bits, tok)
    is_masked = masked > 0.5
    qm, vm = queries[tok : tok + 1], values[tok : tok + 1]
    q_ref[...] = jnp.where(is_masked, qm.astype(F32), queries[:tok].astype(F32)).astype(BF16)
    outs = start_all(
        [
            pltpu.make_async_copy(src, dst, out_sems.at[i])
            for i, (src, dst) in enumerate(((q_ref, q_hbm), (k_ref, k_hbm), (v_ref, v_hbm)))
        ]
    )
    imp = imp_ref[...].astype(F32)
    weight = LEVELS / lev_ref[...].astype(F32) * (imp[0:1] / imp[1:2])
    row, lane = iota((tok, blocks), 0), iota((tok, blocks), 1)
    token_weight = masked * jnp.sum(
        jnp.where(row // BLOCK == lane, jnp.broadcast_to(weight, (tok, blocks)), 0.0),
        axis=1,
        keepdims=True,
    )
    grad = (cot_ref[...].astype(F32) * token_weight).astype(BF16)
    qm_heads = jnp.where(head_of, jnp.broadcast_to(qm.astype(F32), (LANES, width)), 0.0).astype(BF16)
    score = dot_t(keys, qm_heads)
    own, mask_score = score[:tok], score[tok : tok + 1]
    a_ref[...] = own
    back = dot_t(qm_heads, wk_ref[...])[:BLOCK]
    high = back.astype(BF16)
    low = (back - high.astype(F32)).astype(BF16)
    qk_ref[...] = jnp.zeros(qk_ref.shape, BF16)
    qk_ref[0:BLOCK] = high
    qk_ref[BLOCK : 2 * BLOCK] = high
    qk_ref[2 * BLOCK : 3 * BLOCK] = low

    def block_sums(scores, vals):
        by_block = scores.reshape(blocks, BLOCK, LANES)
        top = jnp.max(by_block, axis=1)
        expo = jnp.exp(by_block - top[:, None, :])
        total = jnp.sum(expo, axis=1)
        share = expo * (1.0 / total)[:, None, :]
        wide = dot(share.reshape(tok, LANES).astype(BF16), spread)
        mixed = jnp.sum((wide * vals).reshape(blocks, BLOCK, width), axis=1)
        return top + jnp.log(total), mixed

    value_f = values[:tok].astype(F32)
    top, mixed = block_sums(own, value_f)
    top_n, mixed_n = block_sums(
        jnp.where(is_masked, mask_score, own), jnp.where(is_masked, vm.astype(F32), value_f)
    )
    grad_sum = jnp.sum(grad.astype(F32).reshape(blocks, BLOCK, width), axis=1)
    product = grad_sum * mixed_n
    high = product.astype(BF16)
    low = (product - high.astype(F32)).astype(BF16)
    grad_mix = dot_t(high, spread) + dot_t(low, spread)
    in_heads = iota((blocks, LANES), 1) < HEADS
    packed = jnp.where(in_heads, top, 0.0)
    for place, part in enumerate((top_n, grad_mix)):
        packed = packed + pltpu.roll(jnp.where(in_heads, part, 0.0), 16 * (place + 1), 1)
    high = packed.astype(BF16)
    rest = packed - high.astype(F32)
    mid = rest.astype(BF16)
    low = (rest - mid.astype(F32)).astype(BF16)
    stats_ref[0] = grad_sum.astype(BF16)
    stats_ref[1] = mixed.astype(BF16)
    stats_ref[2] = jnp.zeros((blocks, width), BF16)
    stats_ref[2, :, 0:LANES] = high
    stats_ref[2, :, LANES : 2 * LANES] = mid
    stats_ref[2, :, 2 * LANES : 3 * LANES] = low
    for copy in outs:
        copy.wait()


def grad_kernel(
    place_ref, back_hbm, ahead_hbm, y_hbm, c_hbm, own_hbm, a_hbm, v_hbm, qk_hbm, wv_hbm,
    square_ref, raw_ref,
    held, a_ref, v_ref, qk_ref, wv_ref, dvalues, in_sems,
):
    tok, width = v_ref.shape
    blocks = tok // BLOCK
    mine = place_ref[0]
    last = place_ref[1]
    at = mine % GROUP
    held[...] = jnp.zeros(held.shape, BF16)
    y_side = jnp.where(at & 2 == 0, 0, 2 * GROUP)
    c_side = jnp.where(at & 1 == 0, 0, 2 * GROUP)
    moves = (
        (back_hbm, held.at[at]),
        (own_hbm, held.at[GROUP + at]),
        (ahead_hbm, held.at[2 * GROUP + at]),
        (y_hbm.at[0], held.at[GROUP + (at ^ 2)]),
        (y_hbm.at[1], held.at[y_side + (at ^ 2)]),
        (c_hbm.at[0], held.at[GROUP + (at ^ 1)]),
        (c_hbm.at[1], held.at[c_side + (at ^ 1)]),
        (c_hbm.at[2], held.at[GROUP + (at ^ 3)]),
        (c_hbm.at[3], held.at[y_side + (at ^ 3)]),
        (a_hbm, a_ref),
        (v_hbm, v_ref),
        (qk_hbm, qk_ref),
        (wv_hbm, wv_ref),
    )
    copies = start_all(
        [pltpu.make_async_copy(src, dst, in_sems.at[i]) for i, (src, dst) in enumerate(moves)]
    )
    near = GROUP * blocks
    count_b = 2 * near
    count_u = 3 * near
    pad_u = 4 * near
    first_block = (mine - at - GROUP) * blocks
    u_at = iota((count_u, count_b), 0)
    b_at = iota((count_u, count_b), 1) + near
    seen = (u_at < b_at) & (u_at >= b_at - near) & (u_at + first_block >= 0)
    bias = jnp.where(seen, 0.0, -jnp.inf)
    for copy in copies[:9]:
        copy.wait()
    grads = held[GROUP:, 0].reshape(count_b, width)
    mixed = held[:, 1].reshape(count_u, width)
    scalars = (
        held[:, 2, :, 0:LANES].astype(F32)
        + held[:, 2, :, LANES : 2 * LANES].astype(F32)
        + held[:, 2, :, 2 * LANES : 3 * LANES].astype(F32)
    ).reshape(count_u, LANES)
    padded = jnp.concatenate(
        [scalars[near:], jnp.zeros((pad_u - count_b, LANES), F32)], axis=0
    )
    flipped = padded.T[:, :count_b]
    logs, deltas = [], []
    for pair_at in range(HEADS // 2):
        pair = columns(pair_at, LANES)
        products = dot_t(both_heads(mixed[:, pair]), grads[:, pair])
        for half in range(2):
            h = 2 * pair_at + half
            top = scalars[:, h : h + 1] + bias
            top_n = flipped[16 + h : 17 + h]
            peak = jnp.maximum(jnp.max(top, axis=0, keepdims=True), top_n)
            expo = jnp.exp(top - peak)
            expo_n = jnp.exp(top_n - peak)
            den = jnp.sum(expo, axis=0, keepdims=True) + expo_n
            delta = jnp.sum(expo * products[columns(half, count_u)], axis=0, keepdims=True)
            delta = (delta + expo_n * flipped[32 + h : 33 + h]) / den
            logs.append(peak + jnp.log(den))
            deltas.append(delta)
    own_at = near + at * blocks + iota((tok, count_b), 0) // BLOCK
    b_at = iota((tok, count_b), 1) + near
    seen = (own_at < b_at) & (own_at >= b_at - near) & (b_at + first_block < last)
    bias = jnp.where(seen, 0.0, -jnp.inf)
    lane_u = iota((tok, LANES), 1)
    sigma = jnp.zeros((tok, LANES), F32)
    copies[9].wait()
    copies[10].wait()
    scores = a_ref[...]
    for pair_at in range(HEADS // 2):
        pair = columns(pair_at, LANES)
        grad_pair = grads[:, pair]
        dprobs = dot_t(both_heads(v_ref[:, pair]), grad_pair)
        probs = []
        for half in range(2):
            h = 2 * pair_at + half
            prob = jnp.exp(scores[:, h : h + 1] - logs[h] + bias)
            term = prob * (dprobs[columns(half, tok)] - deltas[h])
            sigma = jnp.where(lane_u == h, jnp.sum(term, axis=1, keepdims=True), sigma)
            probs.append(prob.astype(BF16))
        parts = dot(jnp.concatenate(probs, axis=0), grad_pair)
        dvalues[:, pair] = jnp.where(lane_u < HEAD_DIM, parts[:tok], parts[tok:]).astype(BF16)
    high = sigma.astype(BF16).astype(F32)
    low = (sigma - high).astype(BF16).astype(F32)
    split = (high + pltpu.roll(low, 16, 1) + pltpu.roll(high, 32, 1)).astype(BF16)
    copies[11].wait()
    copies[12].wait()
    raw = dot_t(dvalues[...], wv_ref[...]) + dot(split, qk_ref[...])
    raw_ref[...] = raw
    total = jnp.sum(raw * raw, axis=0, keepdims=True)
    total = jnp.sum(total, axis=1, keepdims=True)
    square_ref[...] = jnp.broadcast_to(total, square_ref.shape)


def own_kernel(
    q_hbm, k_hbm, v_hbm, km_hbm, vm_hbm, bits_hbm,
    log_ref, mixed_ref,
    bits_ref, q_ref, k_ref, v_ref, km_ref, vm_ref, in_sems,
):
    tok, width = q_ref.shape
    pairs = HEADS // 2
    sources = (bits_hbm, q_hbm, k_hbm, v_hbm, km_hbm, vm_hbm)
    targets = (bits_ref, q_ref, k_ref, v_ref, km_ref, vm_ref)
    copies = start_all(
        [
            pltpu.make_async_copy(src, dst, in_sems.at[i])
            for i, (src, dst) in enumerate(zip(sources, targets))
        ]
    )
    copies[0].wait()
    row_b, col_b = iota((tok, tok), 0) // BLOCK, iota((tok, tok), 1) // BLOCK
    masked = token_mask_row(bits_ref[...], tok)
    own_bias = jnp.where((col_b < row_b) | ((col_b == row_b) & (masked < 0.5)), 0.0, -jnp.inf)
    count = jnp.sum(jnp.where(row_b == col_b, masked, 0.0), axis=1, keepdims=True)
    mask_bias = jnp.where(iota((tok, LANES), 1).astype(F32) < count, 0.0, -jnp.inf)
    bias = jnp.concatenate([own_bias, mask_bias], axis=1)
    bias = jnp.concatenate([bias, bias], axis=0)
    lane = iota((tok, LANES), 1)
    logs = jnp.zeros((tok, LANES), F32)
    for copy in copies[1:]:
        copy.wait()
    for pair_at in range(pairs):
        pair = columns(pair_at, LANES)
        k_mask = jnp.broadcast_to(km_ref[0:1, pair], (LANES, LANES))
        v_mask = jnp.broadcast_to(vm_ref[0:1, pair], (LANES, LANES))
        keys = jnp.concatenate([k_ref[:, pair], k_mask], axis=0)
        vals = jnp.concatenate([v_ref[:, pair], v_mask], axis=0)
        score = dot_t(both_heads(q_ref[:, pair]), keys) + bias
        peak = jnp.max(score, axis=1, keepdims=True)
        expo = jnp.exp(score - peak)
        den = jnp.sum(expo, axis=1, keepdims=True)
        mixed = dot(expo.astype(BF16), vals) / den
        log = peak + jnp.log(den)
        logs = jnp.where(lane == 2 * pair_at, log[:tok], logs)
        logs = jnp.where(lane == 2 * pair_at + 1, log[tok:], logs)
        mixed_ref[:, pair] = jnp.where(lane < HEAD_DIM, mixed[:tok], mixed[tok:]).astype(BF16)
    log_ref[...] = logs


def rest_kernel(
    place_ref, far_hbm, two_hbm, one_hbm, three_hbm, q_hbm, mixed_hbm, log_hbm, after_hbm, wk_hbm, wv_hbm,
    out_ref,
    rows, wk_ref, wv_ref, q_ref, mixed_ref, log_ref, keys, vals, total_ref, in_sems,
):
    tok, width = q_ref.shape
    shards = rows.shape[0]
    mine = place_ref[0]
    part = 2 * LANES
    parts = width // part

    def load(src, dst, at):
        return pltpu.make_async_copy(src, dst, in_sems.at[at])

    weights = []
    for at in range(parts):
        cols = columns(at, part)
        for i, (src, dst) in enumerate(((wk_hbm, wk_ref), (wv_hbm, wv_ref))):
            weights.append(load(src.at[:, cols], dst.at[:, cols], shards + 2 * at + i))
    others = [
        load(src, dst, shards + 2 * parts + i)
        for i, (src, dst) in enumerate(((q_hbm, q_ref), (mixed_hbm, mixed_ref), (log_hbm, log_ref)))
    ]
    shard_copies = [
        load(src, rows.at[at], at)
        for at, src in enumerate((far_hbm, two_hbm, one_hbm, three_hbm))
    ]
    start_all(shard_copies[:1])
    start_all(weights[:2])
    start_all(shard_copies[1:])
    start_all(others)
    start_all(weights[2:])
    row_b, col_b = iota((tok, tok), 0) // BLOCK, iota((tok, tok), 1) // BLOCK
    far_bias = jnp.where((col_b >= row_b) & (mine >= GROUP), 0.0, NEVER)
    far_bias = jnp.concatenate([far_bias, far_bias], axis=0)
    biases = [far_bias] + [jnp.where(mine >= back, 0.0, NEVER) for back in (2, 1, 3)]
    lane = iota((tok, LANES), 1)
    for at in range(parts):
        cols = columns(at, part)
        for copy in weights[2 * at : 2 * at + 2]:
            copy.wait()
        for place in range(shards):
            if at == 0:
                shard_copies[place].wait()
            span = columns(place, tok)
            keys[span, cols] = dot(rows[place], wk_ref[:, cols]).astype(BF16)
            vals[span, cols] = dot(rows[place], wv_ref[:, cols]).astype(BF16)
    for copy in others:
        copy.wait()
    logs = jnp.zeros((tok, LANES), F32)
    for pair_at in range(HEADS // 2):
        pair = columns(pair_at, LANES)
        score = dot_t(both_heads(q_ref[:, pair]), keys[:, pair])
        pieces = [score[:, columns(place, tok)] + biases[place] for place in range(shards)]
        peak = jnp.maximum(jnp.maximum(pieces[0], pieces[1]), jnp.maximum(pieces[2], pieces[3]))
        peak = jnp.max(peak, axis=1, keepdims=True)
        pieces = [jnp.exp(piece - peak) for piece in pieces]
        den = jnp.sum((pieces[0] + pieces[1]) + (pieces[2] + pieces[3]), axis=1, keepdims=True)
        expo = jnp.concatenate([piece.astype(BF16) for piece in pieces], axis=1)
        mixed = dot(expo, vals[:, pair]) / den
        log = peak + jnp.log(den)
        logs = jnp.where(lane == 2 * pair_at, log[:tok], logs)
        logs = jnp.where(lane == 2 * pair_at + 1, log[tok:], logs)
        total_ref[:, pair] = jnp.where(lane < HEAD_DIM, mixed[:tok], mixed[tok:])
    share = 1.0 / (1.0 + jnp.exp(logs - log_ref[...]))
    high = share.astype(BF16)
    less = (share - high.astype(F32)).astype(BF16)
    head_of = iota((LANES, width), 1) // HEAD_DIM == iota((LANES, width), 0)
    spread = jnp.where(head_of, 1.0, 0.0).astype(BF16)
    share = dot(high, spread) + dot(less, spread)
    total = total_ref[...]
    out_ref[...] = (total + share * (mixed_ref[...].astype(F32) - total)).astype(BF16)


def scale_kernel(entries, square_ref, raw_ref, out_hbm, out_ref, sems):
    tok = raw_ref.shape[0]
    pieces = 4
    total = jnp.sum(square_ref[:, 0:1], axis=0, keepdims=True)
    rms = jnp.sqrt(total / entries + EPS)
    factor = jnp.minimum(1.0, CLIP / rms)
    outs = []
    for at in range(pieces):
        span = columns(at, tok // pieces)
        out_ref[span] = raw_ref[span] * factor
        outs.append(pltpu.make_async_copy(out_ref.at[span], out_hbm.at[span], sems.at[at]))
        outs[-1].start()
    for copy in outs:
        copy.wait()


def call(kernel, out_shape, hbm_out, args, scratch, smem=(), vmem=(), loose=(), flops=0):
    args = [pltpu.with_memory_space_constraint(array, pltpu.HBM) for array in args]
    args = [*loose, *args, *vmem]
    kinds = [pltpu.SMEM] * len(smem) + [pl.ANY] * (len(args) - len(vmem)) + [pltpu.VMEM] * len(vmem)
    out_kinds = [pltpu.VMEM] * (len(out_shape) - hbm_out) + [pl.ANY] * hbm_out
    return pl.pallas_call(
        kernel,
        out_shape=out_shape,
        in_specs=[pl.BlockSpec(memory_space=kind) for kind in kinds],
        out_specs=[pl.BlockSpec(memory_space=kind) for kind in out_kinds],
        scratch_shapes=scratch,
        compiler_params=pltpu.CompilerParams(vmem_limit_bytes=VMEM_LIMIT),
        cost_estimate=pl.CostEstimate(flops=flops, bytes_accessed=1 << 10, transcendentals=0),
    )(*smem, *args)


def shift(rows, distance):
    devices = range(lax.axis_size("seq"))
    return lax.ppermute(rows, "seq", [(i, i + distance) for i in devices if i + distance in devices])


def swap(rows, bit):
    return lax.ppermute(rows, "seq", [(i, i ^ bit) for i in range(lax.axis_size("seq"))])


def on_device(clean, out_cot, mask_bits, levels, importance, w_query, w_key, w_value, mask_embed):
    clean_rows = clean[0]
    tok, width = clean_rows.shape
    blocks = tok // BLOCK
    place = lax.axis_index("seq")
    count = lax.axis_size("seq")
    parts = lax.axis_size("dp") * count
    where = jnp.stack([place, jnp.int32(count * blocks)]).astype(jnp.int32)
    rows = (tok, width)
    square_w = (width, width)

    def like(*dims, dtype=BF16):
        return jax.ShapeDtypeStruct(dims, dtype)

    def vmem(*dims, dtype=BF16):
        return pltpu.VMEM(dims, dtype)

    def sems(count):
        return pltpu.SemaphoreType.DMA((count,))

    with jax.named_scope("halo"):
        far = shift(clean_rows, GROUP)
    with jax.named_scope("local"):
        ratio = importance[0].T
        stats, a, qk, km, vm, q, k, v = call(
            local_kernel,
            [
                like(3, blocks, width), like(tok, LANES, dtype=F32), like(LANES, width),
                like(BLOCK, width), like(BLOCK, width), like(*rows), like(*rows), like(*rows),
            ],
            3,
            [clean_rows, w_key, w_value, w_query, out_cot[0], mask_embed, mask_bits, levels, ratio],
            [
                vmem(*rows), vmem(*square_w), vmem(*square_w), vmem(*square_w), vmem(*rows),
                vmem(width), vmem(1, blocks, dtype=jnp.int32), vmem(1, blocks, dtype=jnp.int32),
                vmem(2, blocks, dtype=jnp.int32), vmem(*rows), vmem(*rows), vmem(*rows),
                sems(9), sems(3),
            ],
            flops=1_000_000_000,
        )
    with jax.named_scope("halo"):
        back, ahead = shift(stats, GROUP), shift(stats, -GROUP)
    with jax.named_scope("own"):
        log, mixed = call(
            own_kernel,
            [like(tok, LANES, dtype=F32), like(*rows)],
            0,
            [mask_bits],
            [
                vmem(1, blocks, dtype=jnp.int32), vmem(*rows), vmem(*rows), vmem(*rows),
                vmem(BLOCK, width), vmem(BLOCK, width), sems(6),
            ],
            loose=[q, k, v, km, vm],
            flops=1_000_000_000,
        )
    with jax.named_scope("halo"):
        back, ahead, far, log = lax.optimization_barrier((back, ahead, far, log))
        y2 = swap(jnp.stack([stats, jnp.where(place & 2 == 0, ahead, back)]), 2)
        clean_rows, far = lax.optimization_barrier((clean_rows, far))
        two = shift(clean_rows, 2)
        sides = jnp.stack([stats, jnp.where(place & 1 == 0, ahead, back)])
        core4 = swap(jnp.concatenate([sides, y2]), 1)
    with jax.named_scope("grad"):
        square, raw = call(
            grad_kernel,
            [like(parts, LANES, dtype=F32), like(*rows, dtype=F32)],
            0,
            [w_value],
            [
                vmem(3 * GROUP, 3, blocks, width), vmem(tok, LANES, dtype=F32), vmem(*rows),
                vmem(LANES, width), vmem(*square_w), vmem(*rows), sems(13),
            ],
            smem=[where],
            loose=[back, ahead, y2, core4, stats, a, v, qk],
            flops=100_000_000,
        )
        two, square = lax.optimization_barrier((two, square))
        mine = place & 1 == 0
        one = swap(jnp.where(mine, clean_rows, two), 1)
        three = swap(jnp.where(mine, two, far), 1)
        squares = lax.all_to_all(square, ("dp", "seq"), 0, 0)
    with jax.named_scope("rest"):
        (attn,) = call(
            rest_kernel,
            [like(*rows)],
            0,
            [w_key, w_value],
            [
                vmem(GROUP, *rows), vmem(*square_w), vmem(*square_w), vmem(*rows), vmem(*rows),
                vmem(tok, LANES, dtype=F32), vmem(GROUP * tok, width), vmem(GROUP * tok, width),
                vmem(*rows, dtype=F32), sems(GROUP + width // LANES + 3),
            ],
            smem=[where],
            loose=[far, two, one, three, q, mixed, log, square],
            flops=8_000_000_000,
        )
    with jax.named_scope("clip"):
        squares, attn = lax.optimization_barrier((squares, attn))
        entries = float(parts * tok * width)
        (grad,) = call(
            lambda *refs: scale_kernel(entries, *refs),
            [like(*rows, dtype=F32)],
            1,
            [],
            [vmem(*rows, dtype=F32), sems(4)],
            vmem=[squares, raw],
        )
    return attn[None], grad[None]


def solution(mesh):
    in_specs = (
        P("dp", "seq", None),
        P("dp", "seq", None),
        P("dp", "seq"),
        P("dp", "seq"),
        P("dp", "seq", None),
        P(),
        P(),
        P(),
        P(),
    )
    out_specs = (P("dp", "seq", None), P("dp", "seq", None))
    return jax.shard_map(
        on_device, mesh=mesh, in_specs=in_specs, out_specs=out_specs, check_vma=False
    )
```

```python
import math

import jax
import jax.numpy as jnp
from jax import lax
from jax.experimental import pallas as pl
from jax.experimental.pallas import tpu as pltpu
from jax.sharding import PartitionSpec as P

HEADS = 12
HEAD_DIM = 64
BLOCK = 16
WINDOW = 1024
LEVELS = 16
EPS = 1e-06
CLIP = 0.25
LANES = 128
NEVER = -1e30
GROUP = 4
F32 = jnp.float32
BF16 = jnp.bfloat16
VMEM_LIMIT = 32 * 1024 * 1024
SCALE = 1.0 / math.sqrt(HEAD_DIM)


def iota(shape, dim):
    return lax.broadcasted_iota(jnp.int32, shape, dim)


def dot(a, b, precision=None):
    return jnp.dot(a, b, preferred_element_type=F32, precision=precision)


def dot_t(a, b, precision=None):
    return lax.dot_general(
        a, b, (((1,), (1,)), ((), ())), preferred_element_type=F32, precision=precision
    )


def token_mask_col(bits_row, tok):
    blocks = bits_row.shape[1]
    row, lane = iota((tok, blocks), 0), iota((tok, blocks), 1)
    bit = jnp.right_shift(jnp.broadcast_to(bits_row, (tok, blocks)), row % BLOCK) & 1
    return jnp.sum(jnp.where(row // BLOCK == lane, bit, 0).astype(F32), axis=1, keepdims=True)


def token_mask_row(bits_row, tok):
    blocks = bits_row.shape[1]
    diag = iota((blocks, blocks), 0) == iota((blocks, blocks), 1)
    col = jnp.sum(
        jnp.where(diag, jnp.broadcast_to(bits_row, (blocks, blocks)), 0).astype(F32),
        axis=1,
        keepdims=True,
    ).astype(jnp.int32)
    row, lane = iota((blocks, tok), 0), iota((blocks, tok), 1)
    bit = jnp.right_shift(jnp.broadcast_to(col, (blocks, tok)), lane % BLOCK) & 1
    return jnp.sum(jnp.where(lane // BLOCK == row, bit, 0).astype(F32), axis=0, keepdims=True)


def start_all(copies):
    for copy in copies:
        copy.start()
    return copies


def columns(at, count):
    return slice(at * count, (at + 1) * count)


def both_heads(pair):
    low = iota(pair.shape, 1) < HEAD_DIM
    wide = pair.astype(F32)
    return jnp.concatenate([jnp.where(low, wide, 0.0), jnp.where(low, 0.0, wide)], axis=0).astype(BF16)


def local_kernel(
    clean_hbm, wk_hbm, wv_hbm, wq_hbm, cot_hbm, me_hbm, bits_hbm, lev_hbm, imp_hbm,
    stats_ref, a_ref, qk_ref, km_ref, vm_ref, flags_ref, q_ref, k_ref, v_ref,
    clean_ref, wk_ref, wv_ref, wq_ref, cot_ref, me_ref, bits_ref, lev_ref, imp_ref, in_sems,
):
    sources = (clean_hbm, me_hbm, wk_hbm, wv_hbm, wq_hbm, bits_hbm, lev_hbm, imp_hbm, cot_hbm)
    targets = (clean_ref, me_ref, wk_ref, wv_ref, wq_ref, bits_ref, lev_ref, imp_ref, cot_ref)
    copies = start_all(
        [
            pltpu.make_async_copy(src, dst, in_sems.at[i])
            for i, (src, dst) in enumerate(zip(sources, targets))
        ]
    )
    tok, width = clean_ref.shape
    blocks = tok // BLOCK
    head_of = iota((LANES, width), 1) // HEAD_DIM == iota((LANES, width), 0)
    spread = jnp.where(head_of, 1.0, 0.0).astype(BF16)
    copies[0].wait()
    copies[1].wait()
    mask_rows = jnp.broadcast_to(me_ref[...].reshape(1, width), (BLOCK, width))
    rows = jnp.concatenate([clean_ref[...], mask_rows], axis=0)
    copies[2].wait()
    keys = dot(rows, wk_ref[...]).astype(BF16)
    k_ref[...] = keys[:tok]
    km_ref[...] = keys[tok:]
    copies[3].wait()
    values = dot(rows, wv_ref[...]).astype(BF16)
    v_ref[...] = values[:tok]
    vm_ref[...] = values[tok:]
    copies[4].wait()
    queries = (dot(rows, wq_ref[...]).astype(BF16).astype(F32) * SCALE).astype(BF16)
    for copy in copies[5:]:
        copy.wait()
    bits = bits_ref[...]
    masked = token_mask_col(bits, tok)
    is_masked = masked > 0.5
    qm, vm = queries[tok : tok + 1], values[tok : tok + 1]
    q_ref[...] = jnp.where(is_masked, qm.astype(F32), queries[:tok].astype(F32)).astype(BF16)
    flags_ref[...] = jnp.broadcast_to(token_mask_row(bits, tok), flags_ref.shape)
    imp = imp_ref[...].astype(F32)
    weight = LEVELS / lev_ref[...].astype(F32) * (imp[0:1] / imp[1:2])
    row, lane = iota((tok, blocks), 0), iota((tok, blocks), 1)
    token_weight = masked * jnp.sum(
        jnp.where(row // BLOCK == lane, jnp.broadcast_to(weight, (tok, blocks)), 0.0),
        axis=1,
        keepdims=True,
    )
    grad = (cot_ref[...].astype(F32) * token_weight).astype(BF16)
    qm_heads = jnp.where(head_of, jnp.broadcast_to(qm.astype(F32), (LANES, width)), 0.0).astype(BF16)
    score = dot_t(keys, qm_heads)
    own, mask_score = score[:tok], score[tok : tok + 1]
    a_ref[...] = own
    back = dot_t(qm_heads, wk_ref[...])[:BLOCK]
    high = back.astype(BF16)
    low = (back - high.astype(F32)).astype(BF16)
    qk_ref[...] = jnp.zeros(qk_ref.shape, BF16)
    qk_ref[0:BLOCK] = high
    qk_ref[BLOCK : 2 * BLOCK] = high
    qk_ref[2 * BLOCK : 3 * BLOCK] = low

    def block_sums(scores, vals):
        by_block = scores.reshape(blocks, BLOCK, LANES)
        top = jnp.max(by_block, axis=1)
        expo = jnp.exp(by_block - top[:, None, :])
        total = jnp.sum(expo, axis=1)
        share = expo * (1.0 / total)[:, None, :]
        wide = dot(share.reshape(tok, LANES).astype(BF16), spread)
        mixed = jnp.sum((wide * vals).reshape(blocks, BLOCK, width), axis=1)
        return top + jnp.log(total), mixed

    value_f = values[:tok].astype(F32)
    top, mixed = block_sums(own, value_f)
    top_n, mixed_n = block_sums(
        jnp.where(is_masked, mask_score, own), jnp.where(is_masked, vm.astype(F32), value_f)
    )
    grad_sum = jnp.sum(grad.astype(F32).reshape(blocks, BLOCK, width), axis=1)
    product = grad_sum * mixed_n
    high = product.astype(BF16)
    low = (product - high.astype(F32)).astype(BF16)
    grad_mix = dot_t(high, spread) + dot_t(low, spread)
    in_heads = iota((blocks, LANES), 1) < HEADS
    packed = jnp.where(in_heads, top, 0.0)
    for place, part in enumerate((top_n, grad_mix)):
        packed = packed + pltpu.roll(jnp.where(in_heads, part, 0.0), 16 * (place + 1), 1)
    high = packed.astype(BF16)
    rest = packed - high.astype(F32)
    mid = rest.astype(BF16)
    low = (rest - mid.astype(F32)).astype(BF16)
    stats_ref[0] = grad_sum.astype(BF16)
    stats_ref[1] = mixed.astype(BF16)
    stats_ref[2] = jnp.zeros((blocks, width), BF16)
    stats_ref[2, :, 0:LANES] = high
    stats_ref[2, :, LANES : 2 * LANES] = mid
    stats_ref[2, :, 2 * LANES : 3 * LANES] = low


def grad_kernel(
    place_ref, back_hbm, ahead_hbm, y_hbm, c_hbm, own_hbm, wv_hbm, a_ref, v_ref, qk_ref,
    square_ref, raw_ref,
    held, wv_ref, dvalues, in_sems,
):
    tok, width = v_ref.shape
    blocks = tok // BLOCK
    mine = place_ref[0]
    last = place_ref[1]
    at = mine % GROUP
    held[...] = jnp.zeros(held.shape, BF16)
    y_side = jnp.where(at & 2 == 0, 0, 2 * GROUP)
    c_side = jnp.where(at & 1 == 0, 0, 2 * GROUP)
    moves = (
        (back_hbm, held.at[at]),
        (own_hbm, held.at[GROUP + at]),
        (ahead_hbm, held.at[2 * GROUP + at]),
        (y_hbm.at[0], held.at[GROUP + (at ^ 2)]),
        (y_hbm.at[1], held.at[y_side + (at ^ 2)]),
        (c_hbm.at[0], held.at[GROUP + (at ^ 1)]),
        (c_hbm.at[1], held.at[c_side + (at ^ 1)]),
        (c_hbm.at[2], held.at[GROUP + (at ^ 3)]),
        (c_hbm.at[3], held.at[y_side + (at ^ 3)]),
        (wv_hbm, wv_ref),
    )
    copies = start_all(
        [pltpu.make_async_copy(src, dst, in_sems.at[i]) for i, (src, dst) in enumerate(moves)]
    )
    near = GROUP * blocks
    count_b = 2 * near
    count_u = 3 * near
    pad_u = 4 * near
    first_block = (mine - at - GROUP) * blocks
    u_at = iota((count_u, count_b), 0)
    b_at = iota((count_u, count_b), 1) + near
    seen = (u_at < b_at) & (u_at >= b_at - near) & (u_at + first_block >= 0)
    bias = jnp.where(seen, 0.0, -jnp.inf)
    for copy in copies[:9]:
        copy.wait()
    grads = held[GROUP:, 0].reshape(count_b, width)
    mixed = held[:, 1].reshape(count_u, width)
    scalars = (
        held[:, 2, :, 0:LANES].astype(F32)
        + held[:, 2, :, LANES : 2 * LANES].astype(F32)
        + held[:, 2, :, 2 * LANES : 3 * LANES].astype(F32)
    ).reshape(count_u, LANES)
    padded = jnp.concatenate(
        [scalars[near:], jnp.zeros((pad_u - count_b, LANES), F32)], axis=0
    )
    flipped = padded.T[:, :count_b]
    logs, deltas = [], []
    for pair_at in range(HEADS // 2):
        pair = columns(pair_at, LANES)
        products = dot_t(both_heads(mixed[:, pair]), grads[:, pair])
        for half in range(2):
            h = 2 * pair_at + half
            top = scalars[:, h : h + 1] + bias
            top_n = flipped[16 + h : 17 + h]
            peak = jnp.maximum(jnp.max(top, axis=0, keepdims=True), top_n)
            expo = jnp.exp(top - peak)
            expo_n = jnp.exp(top_n - peak)
            den = jnp.sum(expo, axis=0, keepdims=True) + expo_n
            delta = jnp.sum(expo * products[columns(half, count_u)], axis=0, keepdims=True)
            delta = (delta + expo_n * flipped[32 + h : 33 + h]) / den
            logs.append(peak + jnp.log(den))
            deltas.append(delta)
    own_at = near + at * blocks + iota((tok, count_b), 0) // BLOCK
    b_at = iota((tok, count_b), 1) + near
    seen = (own_at < b_at) & (own_at >= b_at - near) & (b_at + first_block < last)
    bias = jnp.where(seen, 0.0, -jnp.inf)
    lane_u = iota((tok, LANES), 1)
    sigma = jnp.zeros((tok, LANES), F32)
    scores = a_ref[...]
    for pair_at in range(HEADS // 2):
        pair = columns(pair_at, LANES)
        grad_pair = grads[:, pair]
        dprobs = dot_t(both_heads(v_ref[:, pair]), grad_pair)
        probs = []
        for half in range(2):
            h = 2 * pair_at + half
            prob = jnp.exp(scores[:, h : h + 1] - logs[h] + bias)
            term = prob * (dprobs[columns(half, tok)] - deltas[h])
            sigma = jnp.where(lane_u == h, jnp.sum(term, axis=1, keepdims=True), sigma)
            probs.append(prob.astype(BF16))
        parts = dot(jnp.concatenate(probs, axis=0), grad_pair)
        dvalues[:, pair] = jnp.where(lane_u < HEAD_DIM, parts[:tok], parts[tok:]).astype(BF16)
    high = sigma.astype(BF16).astype(F32)
    low = (sigma - high).astype(BF16).astype(F32)
    split = (high + pltpu.roll(low, 16, 1) + pltpu.roll(high, 32, 1)).astype(BF16)
    copies[9].wait()
    raw = dot_t(dvalues[...], wv_ref[...]) + dot(split, qk_ref[...])
    raw_ref[...] = raw
    total = jnp.sum(raw * raw, axis=0, keepdims=True)
    total = jnp.sum(total, axis=1, keepdims=True)
    square_ref[...] = jnp.broadcast_to(total, square_ref.shape)


def own_kernel(q_ref, k_ref, v_ref, km_ref, vm_ref, flags_ref, log_ref, mixed_ref):
    tok, width = q_ref.shape
    pairs = HEADS // 2
    row_b, col_b = iota((tok, tok), 0) // BLOCK, iota((tok, tok), 1) // BLOCK
    masked = flags_ref[0:1]
    own_bias = jnp.where((col_b < row_b) | ((col_b == row_b) & (masked < 0.5)), 0.0, -jnp.inf)
    count = jnp.sum(jnp.where(row_b == col_b, masked, 0.0), axis=1, keepdims=True)
    mask_bias = jnp.where(iota((tok, LANES), 1).astype(F32) < count, 0.0, -jnp.inf)
    bias = jnp.concatenate([own_bias, mask_bias], axis=1)
    bias = jnp.concatenate([bias, bias], axis=0)
    lane = iota((tok, LANES), 1)
    logs = jnp.zeros((tok, LANES), F32)
    for pair_at in range(pairs):
        pair = columns(pair_at, LANES)
        k_mask = jnp.broadcast_to(km_ref[0:1, pair], (LANES, LANES))
        v_mask = jnp.broadcast_to(vm_ref[0:1, pair], (LANES, LANES))
        keys = jnp.concatenate([k_ref[:, pair], k_mask], axis=0)
        vals = jnp.concatenate([v_ref[:, pair], v_mask], axis=0)
        score = dot_t(both_heads(q_ref[:, pair]), keys) + bias
        peak = jnp.max(score, axis=1, keepdims=True)
        expo = jnp.exp(score - peak)
        den = jnp.sum(expo, axis=1, keepdims=True)
        mixed = dot(expo.astype(BF16), vals) / den
        log = peak + jnp.log(den)
        logs = jnp.where(lane == 2 * pair_at, log[:tok], logs)
        logs = jnp.where(lane == 2 * pair_at + 1, log[tok:], logs)
        mixed_ref[:, pair] = jnp.where(lane < HEAD_DIM, mixed[:tok], mixed[tok:]).astype(BF16)
    log_ref[...] = logs


def rest_kernel(
    place_ref, after_hbm, mixed_hbm, wk_hbm, wv_hbm,
    far_ref, two_ref, two_over_ref, over_ref, q_ref, log_ref,
    out_ref,
    wk_ref, wv_ref, mixed_ref, keys, vals, total_ref, in_sems,
):
    tok, width = q_ref.shape
    rows = (far_ref, two_ref, two_over_ref, over_ref)
    shards = len(rows)
    mine = place_ref[0]
    part = 2 * LANES
    parts = width // part
    weights = []
    for at in range(parts):
        cols = columns(at, part)
        for i, (src, dst) in enumerate(((wk_hbm, wk_ref), (wv_hbm, wv_ref))):
            weights.append(
                pltpu.make_async_copy(src.at[:, cols], dst.at[:, cols], in_sems.at[2 * at + i])
            )
    start_all(weights)
    mixed_copy = pltpu.make_async_copy(mixed_hbm, mixed_ref, in_sems.at[2 * parts])
    mixed_copy.start()
    row_b, col_b = iota((tok, tok), 0) // BLOCK, iota((tok, tok), 1) // BLOCK
    far_bias = jnp.where((col_b >= row_b) & (mine >= GROUP), 0.0, NEVER)
    far_bias = jnp.concatenate([far_bias, far_bias], axis=0)
    over = jnp.where(mine & 1 == 0, 1, 3)
    biases = [far_bias] + [jnp.where(mine >= back, 0.0, NEVER) for back in (2, over, 4 - over)]
    lane = iota((tok, LANES), 1)

    def project(at):
        cols = columns(at, part)
        for place in range(shards):
            span = columns(place, tok)
            keys[span, cols] = dot(rows[place][...], wk_ref[:, cols]).astype(BF16)
            vals[span, cols] = dot(rows[place][...], wv_ref[:, cols]).astype(BF16)

    def attend(pair_at, logs):
        pair = columns(pair_at, LANES)
        score = dot_t(both_heads(q_ref[:, pair]), keys[:, pair])
        pieces = [score[:, columns(place, tok)] + biases[place] for place in range(shards)]
        peak = jnp.maximum(jnp.maximum(pieces[0], pieces[1]), jnp.maximum(pieces[2], pieces[3]))
        peak = jnp.max(peak, axis=1, keepdims=True)
        pieces = [jnp.exp(piece - peak) for piece in pieces]
        den = jnp.sum((pieces[0] + pieces[1]) + (pieces[2] + pieces[3]), axis=1, keepdims=True)
        expo = jnp.concatenate([piece.astype(BF16) for piece in pieces], axis=1)
        mixed = dot(expo, vals[:, pair]) / den
        total_ref[:, pair] = jnp.where(lane < HEAD_DIM, mixed[:tok], mixed[tok:])
        log = peak + jnp.log(den)
        logs = jnp.where(lane == 2 * pair_at, log[:tok], logs)
        return jnp.where(lane == 2 * pair_at + 1, log[tok:], logs)

    logs = jnp.zeros((tok, LANES), F32)
    for copy in weights[:2]:
        copy.wait()
    project(0)
    for copy in weights[2:]:
        copy.wait()
    for at in range(parts):
        if at + 1 < parts:
            project(at + 1)
        for pair_at in (2 * at, 2 * at + 1):
            logs = attend(pair_at, logs)
    mixed_copy.wait()
    share = 1.0 / (1.0 + jnp.exp(logs - log_ref[...]))
    high = share.astype(BF16)
    less = (share - high.astype(F32)).astype(BF16)
    head_of = iota((LANES, width), 1) // HEAD_DIM == iota((LANES, width), 0)
    spread = jnp.where(head_of, 1.0, 0.0).astype(BF16)
    share = dot(high, spread) + dot(less, spread)
    total = total_ref[...]
    out_ref[...] = (total + share * (mixed_ref[...].astype(F32) - total)).astype(BF16)


def scale_kernel(entries, square_ref, raw_ref, out_hbm, out_ref, sems):
    tok = raw_ref.shape[0]
    pieces = 4
    total = jnp.sum(square_ref[:, 0:1], axis=0, keepdims=True)
    rms = jnp.sqrt(total / entries + EPS)
    factor = jnp.minimum(1.0, CLIP / rms)
    outs = []
    for at in range(pieces):
        span = columns(at, tok // pieces)
        out_ref[span] = raw_ref[span] * factor
        outs.append(pltpu.make_async_copy(out_ref.at[span], out_hbm.at[span], sems.at[at]))
        outs[-1].start()
    for copy in outs:
        copy.wait()


def call(kernel, out_shape, hbm_out, args, scratch, smem=(), vmem=(), loose=(), flops=0):
    args = [pltpu.with_memory_space_constraint(array, pltpu.HBM) for array in args]
    args = [*loose, *args, *vmem]
    kinds = [pltpu.SMEM] * len(smem) + [pl.ANY] * (len(args) - len(vmem)) + [pltpu.VMEM] * len(vmem)
    out_kinds = [pltpu.VMEM] * (len(out_shape) - hbm_out) + [pl.ANY] * hbm_out
    return pl.pallas_call(
        kernel,
        out_shape=out_shape,
        in_specs=[pl.BlockSpec(memory_space=kind) for kind in kinds],
        out_specs=[pl.BlockSpec(memory_space=kind) for kind in out_kinds],
        scratch_shapes=scratch,
        compiler_params=pltpu.CompilerParams(vmem_limit_bytes=VMEM_LIMIT),
        cost_estimate=pl.CostEstimate(flops=flops, bytes_accessed=1 << 10, transcendentals=0),
    )(*smem, *args)


def shift(rows, distance):
    devices = range(lax.axis_size("seq"))
    return lax.ppermute(rows, "seq", [(i, i + distance) for i in devices if i + distance in devices])


def swap(rows, bit):
    return lax.ppermute(rows, "seq", [(i, i ^ bit) for i in range(lax.axis_size("seq"))])


def on_device(clean, out_cot, mask_bits, levels, importance, w_query, w_key, w_value, mask_embed):
    clean_rows = clean[0]
    tok, width = clean_rows.shape
    blocks = tok // BLOCK
    place = lax.axis_index("seq")
    count = lax.axis_size("seq")
    parts = lax.axis_size("dp") * count
    where = jnp.stack([place, jnp.int32(count * blocks)]).astype(jnp.int32)
    rows = (tok, width)
    square_w = (width, width)

    def like(*dims, dtype=BF16):
        return jax.ShapeDtypeStruct(dims, dtype)

    def vmem(*dims, dtype=BF16):
        return pltpu.VMEM(dims, dtype)

    def sems(count):
        return pltpu.SemaphoreType.DMA((count,))

    with jax.named_scope("halo"):
        far = shift(clean_rows, GROUP)
    with jax.named_scope("local"):
        ratio = importance[0].T
        stats, a, qk, km, vm, flags, q, k, v = call(
            local_kernel,
            [
                like(3, blocks, width), like(tok, LANES, dtype=F32), like(LANES, width),
                like(BLOCK, width), like(BLOCK, width), like(8, tok, dtype=F32),
                like(*rows), like(*rows), like(*rows),
            ],
            0,
            [clean_rows, w_key, w_value, w_query, out_cot[0], mask_embed, mask_bits, levels, ratio],
            [
                vmem(*rows), vmem(*square_w), vmem(*square_w), vmem(*square_w), vmem(*rows),
                vmem(width), vmem(1, blocks, dtype=jnp.int32), vmem(1, blocks, dtype=jnp.int32),
                vmem(2, blocks, dtype=jnp.int32), sems(9),
            ],
            flops=1_000_000_000,
        )
    with jax.named_scope("halo"):
        back, ahead = shift(stats, GROUP), shift(stats, -GROUP)
    with jax.named_scope("own"):
        log, mixed = call(
            own_kernel,
            [like(tok, LANES, dtype=F32), like(*rows)],
            0,
            [],
            [],
            vmem=[q, k, v, km, vm, flags],
            flops=1_000_000_000,
        )
    with jax.named_scope("halo"):
        back, ahead, far, log = lax.optimization_barrier((back, ahead, far, log))
        over = swap(jnp.where(place & 1 == 0, clean_rows, far), 1)
        y2 = swap(jnp.stack([stats, jnp.where(place & 2 == 0, ahead, back)]), 2)
        two = swap(jnp.where(place & 2 == 0, clean_rows, far), 2)
        sides = jnp.stack([stats, jnp.where(place & 1 == 0, ahead, back)])
        core4 = swap(jnp.concatenate([sides, y2]), 1)
    with jax.named_scope("grad"):
        square, raw = call(
            grad_kernel,
            [like(parts, LANES, dtype=F32), like(*rows, dtype=F32)],
            0,
            [w_value],
            [
                vmem(3 * GROUP, 3, blocks, width), vmem(*square_w), vmem(*rows), sems(10),
            ],
            smem=[where],
            loose=[back, ahead, y2, core4, stats],
            vmem=[a, v, qk],
            flops=100_000_000,
        )
        two, square = lax.optimization_barrier((two, square))
        two_over = swap(two, 1)
        squares = lax.all_to_all(square, ("dp", "seq"), 0, 0)
    with jax.named_scope("rest"):
        (attn,) = call(
            rest_kernel,
            [like(*rows)],
            0,
            [mixed, w_key, w_value],
            [
                vmem(*square_w), vmem(*square_w), vmem(*rows), vmem(GROUP * tok, width),
                vmem(GROUP * tok, width), vmem(*rows, dtype=F32), sems(width // LANES + 1),
            ],
            smem=[where],
            loose=[square],
            vmem=[far, two, two_over, over, q, log],
            flops=8_000_000_000,
        )
    with jax.named_scope("clip"):
        squares, attn = lax.optimization_barrier((squares, attn))
        entries = float(parts * tok * width)
        (grad,) = call(
            lambda *refs: scale_kernel(entries, *refs),
            [like(*rows, dtype=F32)],
            1,
            [],
            [vmem(*rows, dtype=F32), sems(4)],
            vmem=[squares, raw],
        )
    return attn[None], grad[None]


def solution(mesh):
    in_specs = (
        P("dp", "seq", None),
        P("dp", "seq", None),
        P("dp", "seq"),
        P("dp", "seq"),
        P("dp", "seq", None),
        P(),
        P(),
        P(),
        P(),
    )
    out_specs = (P("dp", "seq", None), P("dp", "seq", None))
    return jax.shard_map(
        on_device, mesh=mesh, in_specs=in_specs, out_specs=out_specs, check_vma=False
    )
```

```python
import math

import jax
import jax.numpy as jnp
from jax import lax
from jax.experimental import pallas as pl
from jax.experimental.pallas import tpu as pltpu
from jax.sharding import PartitionSpec as P

HEADS = 12
HEAD_DIM = 64
BLOCK = 16
WINDOW = 1024
LEVELS = 16
EPS = 1e-06
CLIP = 0.25
LANES = 128
NEVER = -1e30
SCALARS = 48
GROUP = 4
F32 = jnp.float32
BF16 = jnp.bfloat16
VMEM_LIMIT = 32 * 1024 * 1024
SCALE = 1.0 / math.sqrt(HEAD_DIM)


def iota(shape, dim):
    return lax.broadcasted_iota(jnp.int32, shape, dim)


def dot(a, b, precision=None):
    return jnp.dot(a, b, preferred_element_type=F32, precision=precision)


def dot_t(a, b, precision=None):
    return lax.dot_general(
        a, b, (((1,), (1,)), ((), ())), preferred_element_type=F32, precision=precision
    )


def token_mask_col(bits_row, tok):
    blocks = bits_row.shape[1]
    row, lane = iota((tok, blocks), 0), iota((tok, blocks), 1)
    bit = jnp.right_shift(jnp.broadcast_to(bits_row, (tok, blocks)), row % BLOCK) & 1
    return jnp.sum(jnp.where(row // BLOCK == lane, bit, 0).astype(F32), axis=1, keepdims=True)


def token_mask_row(bits_row, tok):
    blocks = bits_row.shape[1]
    diag = iota((blocks, blocks), 0) == iota((blocks, blocks), 1)
    col = jnp.sum(
        jnp.where(diag, jnp.broadcast_to(bits_row, (blocks, blocks)), 0).astype(F32),
        axis=1,
        keepdims=True,
    ).astype(jnp.int32)
    row, lane = iota((blocks, tok), 0), iota((blocks, tok), 1)
    bit = jnp.right_shift(jnp.broadcast_to(col, (blocks, tok)), lane % BLOCK) & 1
    return jnp.sum(jnp.where(lane // BLOCK == row, bit, 0).astype(F32), axis=0, keepdims=True)


def start_all(copies):
    for copy in copies:
        copy.start()
    return copies


def columns(at, count):
    return slice(at * count, (at + 1) * count)


def both_heads(pair):
    low = iota(pair.shape, 1) < HEAD_DIM
    wide = pair.astype(F32)
    return jnp.concatenate([jnp.where(low, wide, 0.0), jnp.where(low, 0.0, wide)], axis=0).astype(BF16)


def head_spread(width):
    return iota((LANES, width), 1) // HEAD_DIM == iota((LANES, width), 0)


def local_kernel(
    clean_hbm, wk_hbm, wv_hbm, wq_hbm, cot_hbm, me_hbm, bits_hbm, lev_hbm, imp_hbm,
    stats_ref, a_ref, qk_ref, km_ref, vm_ref, flags_ref, q_ref, k_ref, v_ref,
    clean_ref, wk_ref, wv_ref, wq_ref, cot_ref, me_ref, bits_ref, lev_ref, imp_ref, in_sems,
):
    sources = (clean_hbm, me_hbm, wk_hbm, wv_hbm, wq_hbm, bits_hbm, lev_hbm, imp_hbm, cot_hbm)
    targets = (clean_ref, me_ref, wk_ref, wv_ref, wq_ref, bits_ref, lev_ref, imp_ref, cot_ref)
    copies = start_all(
        [
            pltpu.make_async_copy(src, dst, in_sems.at[i])
            for i, (src, dst) in enumerate(zip(sources, targets))
        ]
    )
    tok, width = clean_ref.shape
    blocks = tok // BLOCK
    head_of = head_spread(width)
    spread = jnp.where(head_of, 1.0, 0.0).astype(BF16)
    copies[0].wait()
    copies[1].wait()
    mask_rows = jnp.broadcast_to(me_ref[...].reshape(1, width), (BLOCK, width))
    rows = jnp.concatenate([clean_ref[...], mask_rows], axis=0)
    copies[2].wait()
    keys = dot(rows, wk_ref[...]).astype(BF16)
    k_ref[...] = keys[:tok]
    km_ref[...] = keys[tok:]
    copies[3].wait()
    values = dot(rows, wv_ref[...]).astype(BF16)
    v_ref[...] = values[:tok]
    vm_ref[...] = values[tok:]
    copies[4].wait()
    queries = (dot(rows, wq_ref[...]).astype(BF16).astype(F32) * SCALE).astype(BF16)
    for copy in copies[5:]:
        copy.wait()
    bits = bits_ref[...]
    masked = token_mask_col(bits, tok)
    is_masked = masked > 0.5
    qm, vm = queries[tok : tok + 1], values[tok : tok + 1]
    q_ref[...] = jnp.where(is_masked, qm.astype(F32), queries[:tok].astype(F32)).astype(BF16)
    flags_ref[...] = jnp.broadcast_to(token_mask_row(bits, tok), flags_ref.shape)
    imp = imp_ref[...].astype(F32)
    weight = LEVELS / lev_ref[...].astype(F32) * (imp[0:1] / imp[1:2])
    row, lane = iota((tok, blocks), 0), iota((tok, blocks), 1)
    token_weight = masked * jnp.sum(
        jnp.where(row // BLOCK == lane, jnp.broadcast_to(weight, (tok, blocks)), 0.0),
        axis=1,
        keepdims=True,
    )
    grad = (cot_ref[...].astype(F32) * token_weight).astype(BF16)
    qm_heads = jnp.where(head_of, jnp.broadcast_to(qm.astype(F32), (LANES, width)), 0.0).astype(BF16)
    score = dot_t(keys, qm_heads)
    own, mask_score = score[:tok], score[tok : tok + 1]
    a_ref[...] = own
    back = dot_t(qm_heads, wk_ref[...])[:BLOCK]
    high = back.astype(BF16)
    low = (back - high.astype(F32)).astype(BF16)
    qk_ref[...] = jnp.zeros(qk_ref.shape, BF16)
    qk_ref[0:BLOCK] = high
    qk_ref[BLOCK : 2 * BLOCK] = high
    qk_ref[2 * BLOCK : 3 * BLOCK] = low

    def block_sums(scores, vals):
        by_block = scores.reshape(blocks, BLOCK, LANES)
        top = jnp.max(by_block, axis=1)
        expo = jnp.exp(by_block - top[:, None, :])
        total = jnp.sum(expo, axis=1)
        share = expo * (1.0 / total)[:, None, :]
        wide = dot(share.reshape(tok, LANES).astype(BF16), spread)
        mixed = jnp.sum((wide * vals).reshape(blocks, BLOCK, width), axis=1)
        return top + jnp.log(total), mixed

    value_f = values[:tok].astype(F32)
    top, mixed = block_sums(own, value_f)
    top_n, mixed_n = block_sums(
        jnp.where(is_masked, mask_score, own), jnp.where(is_masked, vm.astype(F32), value_f)
    )
    grad_sum = jnp.sum(grad.astype(F32).reshape(blocks, BLOCK, width), axis=1)
    product = grad_sum * mixed_n
    high = product.astype(BF16)
    low = (product - high.astype(F32)).astype(BF16)
    grad_mix = dot_t(high, spread) + dot_t(low, spread)
    in_heads = iota((blocks, LANES), 1) < HEADS
    packed = jnp.where(in_heads, top, 0.0)
    for place, part in enumerate((top_n, grad_mix)):
        packed = packed + pltpu.roll(jnp.where(in_heads, part, 0.0), 16 * (place + 1), 1)
    high = packed.astype(BF16).astype(F32)
    rest = packed - high
    mid = rest.astype(BF16).astype(F32)
    low = rest - mid
    stats_ref[:, 0:width] = grad_sum.astype(BF16)
    stats_ref[:, width : 2 * width] = mixed.astype(BF16)
    stats_ref[:, 2 * width : 2 * width + LANES] = (high + pltpu.roll(mid, SCALARS, 1)).astype(BF16)
    stats_ref[:, 2 * width + LANES :] = low.astype(BF16)


def grad_kernel(
    place_ref, back_hbm, ahead_hbm, y_hbm, c_hbm, own_hbm, wv_hbm, a_ref, v_ref, qk_ref,
    square_ref, raw_ref, wv_ref,
    held, dvalues, in_sems,
):
    tok, width = v_ref.shape
    blocks = tok // BLOCK
    mine = place_ref[0]
    last = place_ref[1]
    at = mine % GROUP
    held[...] = jnp.zeros(held.shape, BF16)
    y_side = jnp.where(at & 2 == 0, 0, 2 * GROUP)
    c_side = jnp.where(at & 1 == 0, 0, 2 * GROUP)
    moves = (
        (back_hbm, held.at[at]),
        (own_hbm, held.at[GROUP + at]),
        (ahead_hbm, held.at[2 * GROUP + at]),
        (y_hbm.at[0], held.at[GROUP + (at ^ 2)]),
        (y_hbm.at[1], held.at[y_side + (at ^ 2)]),
        (c_hbm.at[0], held.at[GROUP + (at ^ 1)]),
        (c_hbm.at[1], held.at[c_side + (at ^ 1)]),
        (c_hbm.at[2], held.at[GROUP + (at ^ 3)]),
        (c_hbm.at[3], held.at[y_side + (at ^ 3)]),
        (wv_hbm, wv_ref),
    )
    copies = start_all(
        [pltpu.make_async_copy(src, dst, in_sems.at[i]) for i, (src, dst) in enumerate(moves)]
    )
    near = GROUP * blocks
    count_b = 2 * near
    count_u = 3 * near
    pad_u = 4 * near
    first_block = (mine - at - GROUP) * blocks
    u_at = iota((count_u, count_b), 0)
    b_at = iota((count_u, count_b), 1) + near
    seen = (u_at < b_at) & (u_at >= b_at - near) & (u_at + first_block >= 0)
    bias = jnp.where(seen, 0.0, -jnp.inf)
    for copy in copies[:9]:
        copy.wait()
    grads = held[GROUP:, :, 0:width].reshape(count_b, width)
    mixed = held[:, :, width : 2 * width].reshape(count_u, width)
    scalars = held[:, :, 2 * width : 2 * width + LANES].astype(F32).reshape(count_u, LANES)
    scalars = scalars + pltpu.roll(scalars, LANES - SCALARS, 1)
    scalars = scalars + held[:, :, 2 * width + LANES :].astype(F32).reshape(count_u, LANES)
    padded = jnp.concatenate(
        [scalars[near:], jnp.zeros((pad_u - count_b, LANES), F32)], axis=0
    )
    flipped = padded.T[:, :count_b]
    logs, deltas = [], []
    for pair_at in range(HEADS // 2):
        pair = columns(pair_at, LANES)
        products = dot_t(both_heads(mixed[:, pair]), grads[:, pair])
        for half in range(2):
            h = 2 * pair_at + half
            top = scalars[:, h : h + 1] + bias
            top_n = flipped[16 + h : 17 + h]
            peak = jnp.maximum(jnp.max(top, axis=0, keepdims=True), top_n)
            expo = jnp.exp(top - peak)
            expo_n = jnp.exp(top_n - peak)
            den = jnp.sum(expo, axis=0, keepdims=True) + expo_n
            delta = jnp.sum(expo * products[columns(half, count_u)], axis=0, keepdims=True)
            delta = (delta + expo_n * flipped[32 + h : 33 + h]) / den
            logs.append(peak + jnp.log(den))
            deltas.append(delta)
    own_at = near + at * blocks + iota((tok, count_b), 0) // BLOCK
    b_at = iota((tok, count_b), 1) + near
    seen = (own_at < b_at) & (own_at >= b_at - near) & (b_at + first_block < last)
    bias = jnp.where(seen, 0.0, -jnp.inf)
    lane_u = iota((tok, LANES), 1)
    sigma = jnp.zeros((tok, LANES), F32)
    scores = a_ref[...]
    for pair_at in range(HEADS // 2):
        pair = columns(pair_at, LANES)
        grad_pair = grads[:, pair]
        dprobs = dot_t(both_heads(v_ref[:, pair]), grad_pair)
        probs = []
        for half in range(2):
            h = 2 * pair_at + half
            prob = jnp.exp(scores[:, h : h + 1] - logs[h] + bias)
            term = prob * (dprobs[columns(half, tok)] - deltas[h])
            sigma = jnp.where(lane_u == h, jnp.sum(term, axis=1, keepdims=True), sigma)
            probs.append(prob.astype(BF16))
        parts = dot(jnp.concatenate(probs, axis=0), grad_pair)
        dvalues[:, pair] = jnp.where(lane_u < HEAD_DIM, parts[:tok], parts[tok:]).astype(BF16)
    high = sigma.astype(BF16).astype(F32)
    low = (sigma - high).astype(BF16).astype(F32)
    split = (high + pltpu.roll(low, 16, 1) + pltpu.roll(high, 32, 1)).astype(BF16)
    copies[9].wait()
    raw = dot_t(dvalues[...], wv_ref[...]) + dot(split, qk_ref[...])
    raw_ref[...] = raw
    total = jnp.sum(raw * raw, axis=0, keepdims=True)
    total = jnp.sum(total, axis=1, keepdims=True)
    square_ref[...] = jnp.broadcast_to(total, square_ref.shape)


def own_kernel(
    wk_hbm, wv_hbm, q_ref, k_ref, v_ref, km_ref, vm_ref, flags_ref,
    log_ref, mixed_ref, wk_ref, wv_ref,
    sems,
):
    tok, width = q_ref.shape
    pairs = HEADS // 2
    copies = start_all(
        [
            pltpu.make_async_copy(src, dst, sems.at[i])
            for i, (src, dst) in enumerate(((wk_hbm, wk_ref), (wv_hbm, wv_ref)))
        ]
    )
    row_b, col_b = iota((tok, tok), 0) // BLOCK, iota((tok, tok), 1) // BLOCK
    masked = flags_ref[0:1]
    own_bias = jnp.where((col_b < row_b) | ((col_b == row_b) & (masked < 0.5)), 0.0, -jnp.inf)
    count = jnp.sum(jnp.where(row_b == col_b, masked, 0.0), axis=1, keepdims=True)
    mask_bias = jnp.where(iota((tok, LANES), 1).astype(F32) < count, 0.0, -jnp.inf)
    bias = jnp.concatenate([own_bias, mask_bias], axis=1)
    bias = jnp.concatenate([bias, bias], axis=0)
    lane = iota((tok, LANES), 1)
    logs = jnp.zeros((tok, LANES), F32)
    for pair_at in range(pairs):
        pair = columns(pair_at, LANES)
        k_mask = jnp.broadcast_to(km_ref[0:1, pair], (LANES, LANES))
        v_mask = jnp.broadcast_to(vm_ref[0:1, pair], (LANES, LANES))
        keys = jnp.concatenate([k_ref[:, pair], k_mask], axis=0)
        vals = jnp.concatenate([v_ref[:, pair], v_mask], axis=0)
        score = dot_t(both_heads(q_ref[:, pair]), keys) + bias
        peak = jnp.max(score, axis=1, keepdims=True)
        expo = jnp.exp(score - peak)
        den = jnp.sum(expo, axis=1, keepdims=True)
        mixed = dot(expo.astype(BF16), vals) / den
        log = peak + jnp.log(den)
        logs = jnp.where(lane == 2 * pair_at, log[:tok], logs)
        logs = jnp.where(lane == 2 * pair_at + 1, log[tok:], logs)
        mixed_ref[:, pair] = jnp.where(lane < HEAD_DIM, mixed[:tok], mixed[tok:]).astype(BF16)
    log_ref[...] = logs
    for copy in copies:
        copy.wait()


def attend_pair(q_pair, keys, vals, biases):
    tok = q_pair.shape[0]
    score = dot_t(both_heads(q_pair), keys)
    pieces = [score[:, columns(place, tok)] + bias for place, bias in enumerate(biases)]
    peak = pieces[0]
    for piece in pieces[1:]:
        peak = jnp.maximum(peak, piece)
    peak = jnp.max(peak, axis=1, keepdims=True)
    pieces = [jnp.exp(piece - peak) for piece in pieces]
    den = pieces[0]
    for piece in pieces[1:]:
        den = den + piece
    den = jnp.sum(den, axis=1, keepdims=True)
    mixed = dot(jnp.concatenate([piece.astype(BF16) for piece in pieces], axis=1), vals) / den
    low = iota((tok, LANES), 1) < HEAD_DIM
    return jnp.where(low, mixed[:tok], mixed[tok:]), peak + jnp.log(den)


def keep_logs(logs, pair_at, log):
    tok = logs.shape[0]
    lane = iota(logs.shape, 1)
    logs = jnp.where(lane == 2 * pair_at, log[:tok], logs)
    return jnp.where(lane == 2 * pair_at + 1, log[tok:], logs)


def blend(logs, total, old_logs, old_mixed):
    share = 1.0 / (1.0 + jnp.exp(logs - old_logs))
    high = share.astype(BF16)
    low = (share - high.astype(F32)).astype(BF16)
    spread = jnp.where(head_spread(total.shape[1]), 1.0, 0.0).astype(BF16)
    share = dot(high, spread) + dot(low, spread)
    return (total + share * (old_mixed.astype(F32) - total)).astype(BF16)


def far_kernel(
    place_ref, far_ref, q_ref, wk_ref, wv_ref, old_log_ref, old_mixed_ref,
    log_ref, mixed_ref,
    total_ref,
):
    tok, width = q_ref.shape
    row_b, col_b = iota((tok, tok), 0) // BLOCK, iota((tok, tok), 1) // BLOCK
    bias = jnp.where((col_b >= row_b) & (place_ref[0] >= GROUP), 0.0, NEVER)
    bias = jnp.concatenate([bias, bias], axis=0)
    keys = dot(far_ref[...], wk_ref[...]).astype(BF16)
    vals = dot(far_ref[...], wv_ref[...]).astype(BF16)
    logs = jnp.zeros((tok, LANES), F32)
    for pair_at in range(HEADS // 2):
        pair = columns(pair_at, LANES)
        mixed, log = attend_pair(q_ref[:, pair], keys[:, pair], vals[:, pair], [bias])
        total_ref[:, pair] = mixed
        logs = keep_logs(logs, pair_at, log)
    old = old_log_ref[...]
    mixed_ref[...] = blend(logs, total_ref[...], old, old_mixed_ref[...])
    top = jnp.maximum(logs, old)
    log_ref[...] = top + jnp.log(jnp.exp(logs - top) + jnp.exp(old - top))


def rest_kernel(
    place_ref, after_hbm, wk_hbm, mixed_hbm,
    two_ref, two_over_ref, over_ref, q_ref, log_ref, wv_ref,
    out_ref,
    wk_ref, mixed_ref, keys, vals, total_ref, in_sems,
):
    tok, width = q_ref.shape
    rows = (two_ref, two_over_ref, over_ref)
    shards = len(rows)
    mine = place_ref[0]
    part = 2 * LANES
    parts = width // part
    key_copy = pltpu.make_async_copy(wk_hbm, wk_ref, in_sems.at[0])
    key_copy.start()
    mixed_copy = pltpu.make_async_copy(mixed_hbm, mixed_ref, in_sems.at[1])
    mixed_copy.start()
    over = jnp.where(mine & 1 == 0, 1, 3)
    biases = [jnp.where(mine >= back, 0.0, NEVER) for back in (2, over, 4 - over)]

    def project(weight, kept):
        for at in range(parts):
            cols = columns(at, part)
            for place in range(shards):
                kept[columns(place, tok), cols] = dot(rows[place][...], weight[:, cols]).astype(BF16)

    project(wv_ref, vals)
    key_copy.wait()
    project(wk_ref, keys)
    logs = jnp.zeros((tok, LANES), F32)
    for pair_at in range(HEADS // 2):
        pair = columns(pair_at, LANES)
        mixed, log = attend_pair(q_ref[:, pair], keys[:, pair], vals[:, pair], biases)
        total_ref[:, pair] = mixed
        logs = keep_logs(logs, pair_at, log)
    mixed_copy.wait()
    out_ref[...] = blend(logs, total_ref[...], log_ref[...], mixed_ref[...])


def scale_kernel(entries, square_ref, raw_ref, out_hbm, out_ref, sems):
    tok = raw_ref.shape[0]
    pieces = 4
    total = jnp.sum(square_ref[:, 0:1], axis=0, keepdims=True)
    rms = jnp.sqrt(total / entries + EPS)
    factor = jnp.minimum(1.0, CLIP / rms)
    outs = []
    for at in range(pieces):
        span = columns(at, tok // pieces)
        out_ref[span] = raw_ref[span] * factor
        outs.append(pltpu.make_async_copy(out_ref.at[span], out_hbm.at[span], sems.at[at]))
        outs[-1].start()
    for copy in outs:
        copy.wait()


def call(kernel, out_shape, hbm_out, args, scratch, smem=(), vmem=(), loose=(), flops=0):
    args = [pltpu.with_memory_space_constraint(array, pltpu.HBM) for array in args]
    args = [*loose, *args, *vmem]
    kinds = [pltpu.SMEM] * len(smem) + [pl.ANY] * (len(args) - len(vmem)) + [pltpu.VMEM] * len(vmem)
    out_kinds = [pltpu.VMEM] * (len(out_shape) - hbm_out) + [pl.ANY] * hbm_out
    return pl.pallas_call(
        kernel,
        out_shape=out_shape,
        in_specs=[pl.BlockSpec(memory_space=kind) for kind in kinds],
        out_specs=[pl.BlockSpec(memory_space=kind) for kind in out_kinds],
        scratch_shapes=scratch,
        compiler_params=pltpu.CompilerParams(vmem_limit_bytes=VMEM_LIMIT),
        cost_estimate=pl.CostEstimate(flops=flops, bytes_accessed=1 << 10, transcendentals=0),
    )(*smem, *args)


def shift(rows, distance):
    devices = range(lax.axis_size("seq"))
    return lax.ppermute(rows, "seq", [(i, i + distance) for i in devices if i + distance in devices])


def swap(rows, bit):
    return lax.ppermute(rows, "seq", [(i, i ^ bit) for i in range(lax.axis_size("seq"))])


def on_device(clean, out_cot, mask_bits, levels, importance, w_query, w_key, w_value, mask_embed):
    clean_rows = clean[0]
    tok, width = clean_rows.shape
    blocks = tok // BLOCK
    place = lax.axis_index("seq")
    count = lax.axis_size("seq")
    parts = lax.axis_size("dp") * count
    where = jnp.stack([place, jnp.int32(count * blocks)]).astype(jnp.int32)
    rows = (tok, width)
    square_w = (width, width)
    packed = 2 * width + 2 * LANES

    def like(*dims, dtype=BF16):
        return jax.ShapeDtypeStruct(dims, dtype)

    def vmem(*dims, dtype=BF16):
        return pltpu.VMEM(dims, dtype)

    def sems(count):
        return pltpu.SemaphoreType.DMA((count,))

    with jax.named_scope("halo"):
        far = shift(clean_rows, GROUP)
    with jax.named_scope("local"):
        ratio = importance[0].T
        stats, a, qk, km, vm, flags, q, k, v = call(
            local_kernel,
            [
                like(blocks, packed), like(tok, LANES, dtype=F32), like(LANES, width),
                like(BLOCK, width), like(BLOCK, width), like(8, tok, dtype=F32),
                like(*rows), like(*rows), like(*rows),
            ],
            0,
            [clean_rows, w_key, w_value, w_query, out_cot[0], mask_embed, mask_bits, levels, ratio],
            [
                vmem(*rows), vmem(*square_w), vmem(*square_w), vmem(*square_w), vmem(*rows),
                vmem(width), vmem(1, blocks, dtype=jnp.int32), vmem(1, blocks, dtype=jnp.int32),
                vmem(2, blocks, dtype=jnp.int32), sems(9),
            ],
            flops=1_000_000_000,
        )
    with jax.named_scope("halo"):
        back, ahead = shift(stats, GROUP), shift(stats, -GROUP)
        other = jnp.where(place & 2 == 0, clean_rows, far)
        q, other = lax.optimization_barrier((q, other))
        two = swap(other, 2)
    with jax.named_scope("own"):
        log, mixed, wk, wv = call(
            own_kernel,
            [like(tok, LANES, dtype=F32), like(*rows), like(*square_w), like(*square_w)],
            0,
            [w_key, w_value],
            [sems(2)],
            vmem=[q, k, v, km, vm, flags],
            flops=1_000_000_000,
        )
    with jax.named_scope("halo"):
        back, ahead, log = lax.optimization_barrier((back, ahead, log))
        over = swap(jnp.where(place & 1 == 0, clean_rows, far), 1)
        y2 = swap(jnp.stack([stats, jnp.where(place & 2 == 0, ahead, back)]), 2)
    with jax.named_scope("far"):
        log, mixed = call(
            far_kernel,
            [like(tok, LANES, dtype=F32), like(*rows)],
            0,
            [],
            [vmem(*rows, dtype=F32)],
            smem=[where],
            vmem=[far, q, wk, wv, log, mixed],
            flops=100_000_000,
        )
    with jax.named_scope("halo"):
        y2, log = lax.optimization_barrier((y2, log))
        sides = jnp.stack([stats, jnp.where(place & 1 == 0, ahead, back)])
        core4 = swap(jnp.concatenate([sides, y2]), 1)
    with jax.named_scope("grad"):
        square, raw, wv = call(
            grad_kernel,
            [like(parts, LANES, dtype=F32), like(*rows, dtype=F32), like(*square_w)],
            0,
            [w_value],
            [vmem(3 * GROUP, blocks, packed), vmem(*rows), sems(10)],
            smem=[where],
            loose=[back, ahead, y2, core4, stats],
            vmem=[a, v, qk],
            flops=100_000_000,
        )
        two, square = lax.optimization_barrier((two, square))
        two_over = swap(two, 1)
        squares = lax.all_to_all(square, ("dp", "seq"), 0, 0)
    with jax.named_scope("rest"):
        (attn,) = call(
            rest_kernel,
            [like(*rows)],
            0,
            [w_key, mixed],
            [
                vmem(*square_w), vmem(*rows), vmem(3 * tok, width), vmem(3 * tok, width),
                vmem(*rows, dtype=F32), sems(2),
            ],
            smem=[where],
            loose=[square],
            vmem=[two, two_over, over, q, log, wv],
            flops=8_000_000_000,
        )
    with jax.named_scope("clip"):
        squares, attn = lax.optimization_barrier((squares, attn))
        entries = float(parts * tok * width)
        (grad,) = call(
            lambda *refs: scale_kernel(entries, *refs),
            [like(*rows, dtype=F32)],
            1,
            [],
            [vmem(*rows, dtype=F32), sems(4)],
            vmem=[squares, raw],
        )
    return attn[None], grad[None]


def solution(mesh):
    in_specs = (
        P("dp", "seq", None),
        P("dp", "seq", None),
        P("dp", "seq"),
        P("dp", "seq"),
        P("dp", "seq", None),
        P(),
        P(),
        P(),
        P(),
    )
    out_specs = (P("dp", "seq", None), P("dp", "seq", None))
    return jax.shard_map(
        on_device, mesh=mesh, in_specs=in_specs, out_specs=out_specs, check_vma=False
    )
```

```python
import math

import jax
import jax.numpy as jnp
from jax import lax
from jax.experimental import pallas as pl
from jax.experimental.pallas import tpu as pltpu
from jax.sharding import PartitionSpec as P

HEADS = 12
HEAD_DIM = 64
BLOCK = 16
WINDOW = 1024
LEVELS = 16
EPS = 1e-06
CLIP = 0.25
LANES = 128
NEVER = -1e30
SCALARS = 48
GROUP = 4
F32 = jnp.float32
BF16 = jnp.bfloat16
VMEM_LIMIT = 32 * 1024 * 1024
SCALE = 1.0 / math.sqrt(HEAD_DIM)


def iota(shape, dim):
    return lax.broadcasted_iota(jnp.int32, shape, dim)


def dot(a, b, precision=None):
    return jnp.dot(a, b, preferred_element_type=F32, precision=precision)


def dot_t(a, b, precision=None):
    return lax.dot_general(
        a, b, (((1,), (1,)), ((), ())), preferred_element_type=F32, precision=precision
    )


def token_mask_col(bits_row, tok):
    blocks = bits_row.shape[1]
    row, lane = iota((tok, blocks), 0), iota((tok, blocks), 1)
    bit = jnp.right_shift(jnp.broadcast_to(bits_row, (tok, blocks)), row % BLOCK) & 1
    return jnp.sum(jnp.where(row // BLOCK == lane, bit, 0).astype(F32), axis=1, keepdims=True)


def token_mask_row(bits_row, tok):
    blocks = bits_row.shape[1]
    diag = iota((blocks, blocks), 0) == iota((blocks, blocks), 1)
    col = jnp.sum(
        jnp.where(diag, jnp.broadcast_to(bits_row, (blocks, blocks)), 0).astype(F32),
        axis=1,
        keepdims=True,
    ).astype(jnp.int32)
    row, lane = iota((blocks, tok), 0), iota((blocks, tok), 1)
    bit = jnp.right_shift(jnp.broadcast_to(col, (blocks, tok)), lane % BLOCK) & 1
    return jnp.sum(jnp.where(lane // BLOCK == row, bit, 0).astype(F32), axis=0, keepdims=True)


def start_all(copies):
    for copy in copies:
        copy.start()
    return copies


def columns(at, count):
    return slice(at * count, (at + 1) * count)


def both_heads(pair):
    low = iota(pair.shape, 1) < HEAD_DIM
    wide = pair.astype(F32)
    return jnp.concatenate([jnp.where(low, wide, 0.0), jnp.where(low, 0.0, wide)], axis=0).astype(BF16)


def head_spread(width):
    return iota((LANES, width), 1) // HEAD_DIM == iota((LANES, width), 0)


def local_kernel(
    clean_hbm, wk_hbm, wv_hbm, wq_hbm, cot_hbm, me_hbm, bits_hbm, lev_hbm, imp_hbm,
    stats_ref, a_ref, qk_ref, km_ref, vm_ref, flags_ref, q_ref, k_ref, v_ref,
    clean_ref, wk_ref, wv_ref, wq_ref, cot_ref, me_ref, bits_ref, lev_ref, imp_ref, in_sems,
):
    sources = (clean_hbm, me_hbm, wk_hbm, wv_hbm, wq_hbm, bits_hbm, lev_hbm, imp_hbm, cot_hbm)
    targets = (clean_ref, me_ref, wk_ref, wv_ref, wq_ref, bits_ref, lev_ref, imp_ref, cot_ref)
    copies = start_all(
        [
            pltpu.make_async_copy(src, dst, in_sems.at[i])
            for i, (src, dst) in enumerate(zip(sources, targets))
        ]
    )
    tok, width = clean_ref.shape
    blocks = tok // BLOCK
    head_of = head_spread(width)
    spread = jnp.where(head_of, 1.0, 0.0).astype(BF16)
    copies[0].wait()
    copies[1].wait()
    mask_rows = jnp.broadcast_to(me_ref[...].reshape(1, width), (BLOCK, width))
    rows = jnp.concatenate([clean_ref[...], mask_rows], axis=0)
    copies[2].wait()
    keys = dot(rows, wk_ref[...]).astype(BF16)
    k_ref[...] = keys[:tok]
    km_ref[...] = keys[tok:]
    copies[3].wait()
    values = dot(rows, wv_ref[...]).astype(BF16)
    v_ref[...] = values[:tok]
    vm_ref[...] = values[tok:]
    copies[4].wait()
    queries = (dot(rows, wq_ref[...]).astype(BF16).astype(F32) * SCALE).astype(BF16)
    for copy in copies[5:]:
        copy.wait()
    bits = bits_ref[...]
    masked = token_mask_col(bits, tok)
    is_masked = masked > 0.5
    qm, vm = queries[tok : tok + 1], values[tok : tok + 1]
    q_ref[...] = jnp.where(is_masked, qm.astype(F32), queries[:tok].astype(F32)).astype(BF16)
    flags_ref[...] = jnp.broadcast_to(token_mask_row(bits, tok), flags_ref.shape)
    imp = imp_ref[...].astype(F32)
    weight = LEVELS / lev_ref[...].astype(F32) * (imp[0:1] / imp[1:2])
    row, lane = iota((tok, blocks), 0), iota((tok, blocks), 1)
    token_weight = masked * jnp.sum(
        jnp.where(row // BLOCK == lane, jnp.broadcast_to(weight, (tok, blocks)), 0.0),
        axis=1,
        keepdims=True,
    )
    grad = (cot_ref[...].astype(F32) * token_weight).astype(BF16)
    qm_heads = jnp.where(head_of, jnp.broadcast_to(qm.astype(F32), (LANES, width)), 0.0).astype(BF16)
    score = dot_t(keys, qm_heads)
    own, mask_score = score[:tok], score[tok : tok + 1]
    a_ref[...] = own
    back = dot_t(qm_heads, wk_ref[...])[:BLOCK]
    high = back.astype(BF16)
    low = (back - high.astype(F32)).astype(BF16)
    qk_ref[...] = jnp.zeros(qk_ref.shape, BF16)
    qk_ref[0:BLOCK] = high
    qk_ref[BLOCK : 2 * BLOCK] = high
    qk_ref[2 * BLOCK : 3 * BLOCK] = low

    def block_sums(scores, vals):
        by_block = scores.reshape(blocks, BLOCK, LANES)
        top = jnp.max(by_block, axis=1)
        expo = jnp.exp(by_block - top[:, None, :])
        total = jnp.sum(expo, axis=1)
        share = expo * (1.0 / total)[:, None, :]
        wide = dot(share.reshape(tok, LANES).astype(BF16), spread)
        mixed = jnp.sum((wide * vals).reshape(blocks, BLOCK, width), axis=1)
        return top + jnp.log(total), mixed

    value_f = values[:tok].astype(F32)
    top, mixed = block_sums(own, value_f)
    top_n, mixed_n = block_sums(
        jnp.where(is_masked, mask_score, own), jnp.where(is_masked, vm.astype(F32), value_f)
    )
    grad_sum = jnp.sum(grad.astype(F32).reshape(blocks, BLOCK, width), axis=1)
    product = grad_sum * mixed_n
    high = product.astype(BF16)
    low = (product - high.astype(F32)).astype(BF16)
    grad_mix = dot_t(high, spread) + dot_t(low, spread)
    in_heads = iota((blocks, LANES), 1) < HEADS
    packed = jnp.where(in_heads, top, 0.0)
    for place, part in enumerate((top_n, grad_mix)):
        packed = packed + pltpu.roll(jnp.where(in_heads, part, 0.0), 16 * (place + 1), 1)
    high = packed.astype(BF16).astype(F32)
    rest = packed - high
    mid = rest.astype(BF16).astype(F32)
    low = rest - mid
    stats_ref[:, 0:width] = grad_sum.astype(BF16)
    stats_ref[:, width : 2 * width] = mixed.astype(BF16)
    stats_ref[:, 2 * width : 2 * width + LANES] = (high + pltpu.roll(mid, SCALARS, 1)).astype(BF16)
    stats_ref[:, 2 * width + LANES :] = low.astype(BF16)


def grad_kernel(
    place_ref, back_hbm, ahead_hbm, y_hbm, c_hbm, own_hbm, wv_hbm, a_ref, v_ref, qk_ref,
    square_ref, raw_ref, wv_ref,
    held, dvalues, in_sems,
):
    tok, width = v_ref.shape
    blocks = tok // BLOCK
    mine = place_ref[0]
    last = place_ref[1]
    at = mine % GROUP
    held[...] = jnp.zeros(held.shape, BF16)
    y_side = jnp.where(at & 2 == 0, 0, 2 * GROUP)
    c_side = jnp.where(at & 1 == 0, 0, 2 * GROUP)
    moves = (
        (back_hbm, held.at[at]),
        (own_hbm, held.at[GROUP + at]),
        (ahead_hbm, held.at[2 * GROUP + at]),
        (y_hbm.at[0], held.at[GROUP + (at ^ 2)]),
        (y_hbm.at[1], held.at[y_side + (at ^ 2)]),
        (c_hbm.at[0], held.at[GROUP + (at ^ 1)]),
        (c_hbm.at[1], held.at[c_side + (at ^ 1)]),
        (c_hbm.at[2], held.at[GROUP + (at ^ 3)]),
        (c_hbm.at[3], held.at[y_side + (at ^ 3)]),
        (wv_hbm, wv_ref),
    )
    copies = start_all(
        [pltpu.make_async_copy(src, dst, in_sems.at[i]) for i, (src, dst) in enumerate(moves)]
    )
    near = GROUP * blocks
    count_b = 2 * near
    count_u = 3 * near
    pad_u = 4 * near
    first_block = (mine - at - GROUP) * blocks
    u_at = iota((count_u, count_b), 0)
    b_at = iota((count_u, count_b), 1) + near
    seen = (u_at < b_at) & (u_at >= b_at - near) & (u_at + first_block >= 0)
    bias = jnp.where(seen, 0.0, -jnp.inf)
    for copy in copies[:9]:
        copy.wait()
    grads = held[GROUP:, :, 0:width].reshape(count_b, width)
    mixed = held[:, :, width : 2 * width].reshape(count_u, width)
    scalars = held[:, :, 2 * width : 2 * width + LANES].astype(F32).reshape(count_u, LANES)
    scalars = scalars + pltpu.roll(scalars, LANES - SCALARS, 1)
    scalars = scalars + held[:, :, 2 * width + LANES :].astype(F32).reshape(count_u, LANES)
    padded = jnp.concatenate(
        [scalars[near:], jnp.zeros((pad_u - count_b, LANES), F32)], axis=0
    )
    flipped = padded.T[:, :count_b]
    logs, deltas = [], []
    for pair_at in range(HEADS // 2):
        pair = columns(pair_at, LANES)
        products = dot_t(both_heads(mixed[:, pair]), grads[:, pair])
        for half in range(2):
            h = 2 * pair_at + half
            top = scalars[:, h : h + 1] + bias
            top_n = flipped[16 + h : 17 + h]
            peak = jnp.maximum(jnp.max(top, axis=0, keepdims=True), top_n)
            expo = jnp.exp(top - peak)
            expo_n = jnp.exp(top_n - peak)
            den = jnp.sum(expo, axis=0, keepdims=True) + expo_n
            delta = jnp.sum(expo * products[columns(half, count_u)], axis=0, keepdims=True)
            delta = (delta + expo_n * flipped[32 + h : 33 + h]) / den
            logs.append(peak + jnp.log(den))
            deltas.append(delta)
    own_at = near + at * blocks + iota((tok, count_b), 0) // BLOCK
    b_at = iota((tok, count_b), 1) + near
    seen = (own_at < b_at) & (own_at >= b_at - near) & (b_at + first_block < last)
    bias = jnp.where(seen, 0.0, -jnp.inf)
    lane_u = iota((tok, LANES), 1)
    terms = []
    scores = a_ref[...]
    for pair_at in range(HEADS // 2):
        pair = columns(pair_at, LANES)
        grad_pair = grads[:, pair]
        dprobs = dot_t(both_heads(v_ref[:, pair]), grad_pair)
        probs = []
        for half in range(2):
            h = 2 * pair_at + half
            prob = jnp.exp(scores[:, h : h + 1] - logs[h] + bias)
            term = prob * (dprobs[columns(half, tok)] - deltas[h])
            terms.append(term.astype(BF16))
            probs.append(prob.astype(BF16))
        parts = dot(jnp.concatenate(probs, axis=0), grad_pair)
        dvalues[:, pair] = jnp.where(lane_u < HEAD_DIM, parts[:tok], parts[tok:]).astype(BF16)
    to_head = iota((HEADS * count_b, LANES), 0) // count_b == iota((HEADS * count_b, LANES), 1)
    sigma = dot(jnp.concatenate(terms, axis=1), jnp.where(to_head, 1.0, 0.0).astype(BF16))
    high = sigma.astype(BF16).astype(F32)
    low = (sigma - high).astype(BF16).astype(F32)
    split = (high + pltpu.roll(low, 16, 1) + pltpu.roll(high, 32, 1)).astype(BF16)
    copies[9].wait()
    raw = dot_t(dvalues[...], wv_ref[...]) + dot(split, qk_ref[...])
    raw_ref[...] = raw
    total = jnp.sum(raw * raw, axis=0, keepdims=True)
    total = jnp.sum(total, axis=1, keepdims=True)
    square_ref[...] = jnp.broadcast_to(total, square_ref.shape)


def own_kernel(
    wk_hbm, wv_hbm, q_ref, k_ref, v_ref, km_ref, vm_ref, flags_ref,
    log_ref, mixed_ref, wk_ref, wv_ref,
    sems,
):
    tok, width = q_ref.shape
    pairs = HEADS // 2
    copies = start_all(
        [
            pltpu.make_async_copy(src, dst, sems.at[i])
            for i, (src, dst) in enumerate(((wk_hbm, wk_ref), (wv_hbm, wv_ref)))
        ]
    )
    row_b, col_b = iota((tok, tok), 0) // BLOCK, iota((tok, tok), 1) // BLOCK
    masked = flags_ref[0:1]
    own_bias = jnp.where((col_b < row_b) | ((col_b == row_b) & (masked < 0.5)), 0.0, -jnp.inf)
    count = jnp.sum(jnp.where(row_b == col_b, masked, 0.0), axis=1, keepdims=True)
    mask_bias = jnp.where(iota((tok, LANES), 1).astype(F32) < count, 0.0, -jnp.inf)
    bias = jnp.concatenate([own_bias, mask_bias], axis=1)
    bias = jnp.concatenate([bias, bias], axis=0)
    lane = iota((tok, LANES), 1)
    logs = jnp.zeros((tok, LANES), F32)
    for pair_at in range(pairs):
        pair = columns(pair_at, LANES)
        k_mask = jnp.broadcast_to(km_ref[0:1, pair], (LANES, LANES))
        v_mask = jnp.broadcast_to(vm_ref[0:1, pair], (LANES, LANES))
        keys = jnp.concatenate([k_ref[:, pair], k_mask], axis=0)
        vals = jnp.concatenate([v_ref[:, pair], v_mask], axis=0)
        score = dot_t(both_heads(q_ref[:, pair]), keys) + bias
        peak = jnp.max(score, axis=1, keepdims=True)
        expo = jnp.exp(score - peak)
        den = jnp.sum(expo, axis=1, keepdims=True)
        mixed = dot(expo.astype(BF16), vals) / den
        log = peak + jnp.log(den)
        logs = jnp.where(lane == 2 * pair_at, log[:tok], logs)
        logs = jnp.where(lane == 2 * pair_at + 1, log[tok:], logs)
        mixed_ref[:, pair] = jnp.where(lane < HEAD_DIM, mixed[:tok], mixed[tok:]).astype(BF16)
    log_ref[...] = logs
    for copy in copies:
        copy.wait()


def attend_pair(q_pair, keys, vals, biases):
    tok = q_pair.shape[0]
    score = dot_t(both_heads(q_pair), keys)
    pieces = [score[:, columns(place, tok)] + bias for place, bias in enumerate(biases)]
    peak = pieces[0]
    for piece in pieces[1:]:
        peak = jnp.maximum(peak, piece)
    peak = jnp.max(peak, axis=1, keepdims=True)
    expo = jnp.concatenate([jnp.exp(piece - peak).astype(BF16) for piece in pieces], axis=1)
    mixed = dot(expo, jnp.concatenate([vals, jnp.ones(vals.shape, BF16)], axis=1))
    mixed, den = mixed[:, :LANES] / mixed[:, LANES:], mixed[:, LANES:]
    low = iota((tok, LANES), 1) < HEAD_DIM
    return jnp.where(low, mixed[:tok], mixed[tok:]), peak + jnp.log(den)


def keep_logs(logs, pair_at, log):
    tok = logs.shape[0]
    lane = iota(logs.shape, 1)
    logs = jnp.where(lane == 2 * pair_at, log[:tok], logs)
    return jnp.where(lane == 2 * pair_at + 1, log[tok:], logs)


def blend(logs, total, old_logs, old_mixed):
    share = 1.0 / (1.0 + jnp.exp(logs - old_logs))
    high = share.astype(BF16)
    low = (share - high.astype(F32)).astype(BF16)
    spread = jnp.where(head_spread(total.shape[1]), 1.0, 0.0).astype(BF16)
    share = dot(high, spread) + dot(low, spread)
    return (total + share * (old_mixed.astype(F32) - total)).astype(BF16)


def far_kernel(
    place_ref, far_ref, q_ref, wk_ref, wv_ref, old_log_ref, old_mixed_ref,
    log_ref, mixed_ref,
    total_ref,
):
    tok, width = q_ref.shape
    row_b, col_b = iota((tok, tok), 0) // BLOCK, iota((tok, tok), 1) // BLOCK
    bias = jnp.where((col_b >= row_b) & (place_ref[0] >= GROUP), 0.0, NEVER)
    bias = jnp.concatenate([bias, bias], axis=0)
    keys = dot(far_ref[...], wk_ref[...]).astype(BF16)
    vals = dot(far_ref[...], wv_ref[...]).astype(BF16)
    logs = jnp.zeros((tok, LANES), F32)
    for pair_at in range(HEADS // 2):
        pair = columns(pair_at, LANES)
        mixed, log = attend_pair(q_ref[:, pair], keys[:, pair], vals[:, pair], [bias])
        total_ref[:, pair] = mixed
        logs = keep_logs(logs, pair_at, log)
    old = old_log_ref[...]
    mixed_ref[...] = blend(logs, total_ref[...], old, old_mixed_ref[...])
    top = jnp.maximum(logs, old)
    log_ref[...] = top + jnp.log(jnp.exp(logs - top) + jnp.exp(old - top))


def rest_kernel(
    place_ref, after_hbm, wk_hbm, mixed_hbm,
    two_ref, two_over_ref, over_ref, q_ref, log_ref, wv_ref,
    out_ref,
    wk_ref, mixed_ref, keys, vals, total_ref, in_sems,
):
    tok, width = q_ref.shape
    rows = (two_ref, two_over_ref, over_ref)
    shards = len(rows)
    mine = place_ref[0]
    part = 2 * LANES
    parts = width // part
    key_copy = pltpu.make_async_copy(wk_hbm, wk_ref, in_sems.at[0])
    key_copy.start()
    mixed_copy = pltpu.make_async_copy(mixed_hbm, mixed_ref, in_sems.at[1])
    mixed_copy.start()
    over = jnp.where(mine & 1 == 0, 1, 3)
    biases = [jnp.where(mine >= back, 0.0, NEVER) for back in (2, over, 4 - over)]

    def project(weight, kept):
        for at in range(parts):
            cols = columns(at, part)
            for place in range(shards):
                kept[columns(place, tok), cols] = dot(rows[place][...], weight[:, cols]).astype(BF16)

    project(wv_ref, vals)
    key_copy.wait()
    project(wk_ref, keys)
    logs = jnp.zeros((tok, LANES), F32)
    for pair_at in range(HEADS // 2):
        pair = columns(pair_at, LANES)
        mixed, log = attend_pair(q_ref[:, pair], keys[:, pair], vals[:, pair], biases)
        total_ref[:, pair] = mixed
        logs = keep_logs(logs, pair_at, log)
    mixed_copy.wait()
    out_ref[...] = blend(logs, total_ref[...], log_ref[...], mixed_ref[...])


def scale_kernel(entries, square_ref, raw_ref, out_hbm, out_ref, sems):
    tok = raw_ref.shape[0]
    pieces = 4
    total = jnp.sum(square_ref[:, 0:1], axis=0, keepdims=True)
    rms = jnp.sqrt(total / entries + EPS)
    factor = jnp.minimum(1.0, CLIP / rms)
    outs = []
    for at in range(pieces):
        span = columns(at, tok // pieces)
        out_ref[span] = raw_ref[span] * factor
        outs.append(pltpu.make_async_copy(out_ref.at[span], out_hbm.at[span], sems.at[at]))
        outs[-1].start()
    for copy in outs:
        copy.wait()


def call(kernel, out_shape, hbm_out, args, scratch, smem=(), vmem=(), loose=(), flops=0):
    args = [pltpu.with_memory_space_constraint(array, pltpu.HBM) for array in args]
    args = [*loose, *args, *vmem]
    kinds = [pltpu.SMEM] * len(smem) + [pl.ANY] * (len(args) - len(vmem)) + [pltpu.VMEM] * len(vmem)
    out_kinds = [pltpu.VMEM] * (len(out_shape) - hbm_out) + [pl.ANY] * hbm_out
    return pl.pallas_call(
        kernel,
        out_shape=out_shape,
        in_specs=[pl.BlockSpec(memory_space=kind) for kind in kinds],
        out_specs=[pl.BlockSpec(memory_space=kind) for kind in out_kinds],
        scratch_shapes=scratch,
        compiler_params=pltpu.CompilerParams(vmem_limit_bytes=VMEM_LIMIT),
        cost_estimate=pl.CostEstimate(flops=flops, bytes_accessed=1 << 10, transcendentals=0),
    )(*smem, *args)


def shift(rows, distance):
    devices = range(lax.axis_size("seq"))
    return lax.ppermute(rows, "seq", [(i, i + distance) for i in devices if i + distance in devices])


def swap(rows, bit):
    return lax.ppermute(rows, "seq", [(i, i ^ bit) for i in range(lax.axis_size("seq"))])


def on_device(clean, out_cot, mask_bits, levels, importance, w_query, w_key, w_value, mask_embed):
    clean_rows = clean[0]
    tok, width = clean_rows.shape
    blocks = tok // BLOCK
    place = lax.axis_index("seq")
    count = lax.axis_size("seq")
    parts = lax.axis_size("dp") * count
    where = jnp.stack([place, jnp.int32(count * blocks)]).astype(jnp.int32)
    rows = (tok, width)
    square_w = (width, width)
    packed = 2 * width + 2 * LANES

    def like(*dims, dtype=BF16):
        return jax.ShapeDtypeStruct(dims, dtype)

    def vmem(*dims, dtype=BF16):
        return pltpu.VMEM(dims, dtype)

    def sems(count):
        return pltpu.SemaphoreType.DMA((count,))

    with jax.named_scope("halo"):
        far = shift(clean_rows, GROUP)
    with jax.named_scope("local"):
        ratio = importance[0].T
        stats, a, qk, km, vm, flags, q, k, v = call(
            local_kernel,
            [
                like(blocks, packed), like(tok, LANES, dtype=F32), like(LANES, width),
                like(BLOCK, width), like(BLOCK, width), like(8, tok, dtype=F32),
                like(*rows), like(*rows), like(*rows),
            ],
            0,
            [clean_rows, w_key, w_value, w_query, out_cot[0], mask_embed, mask_bits, levels, ratio],
            [
                vmem(*rows), vmem(*square_w), vmem(*square_w), vmem(*square_w), vmem(*rows),
                vmem(width), vmem(1, blocks, dtype=jnp.int32), vmem(1, blocks, dtype=jnp.int32),
                vmem(2, blocks, dtype=jnp.int32), sems(9),
            ],
            flops=1_000_000_000,
        )
    with jax.named_scope("halo"):
        back, ahead = shift(stats, GROUP), shift(stats, -GROUP)
        other = jnp.where(place & 2 == 0, clean_rows, far)
        q, other = lax.optimization_barrier((q, other))
        two = swap(other, 2)
    with jax.named_scope("own"):
        log, mixed, wk, wv = call(
            own_kernel,
            [like(tok, LANES, dtype=F32), like(*rows), like(*square_w), like(*square_w)],
            0,
            [w_key, w_value],
            [sems(2)],
            vmem=[q, k, v, km, vm, flags],
            flops=1_000_000_000,
        )
    with jax.named_scope("halo"):
        back, ahead, log = lax.optimization_barrier((back, ahead, log))
        over = swap(jnp.where(place & 1 == 0, clean_rows, far), 1)
        y2 = swap(jnp.stack([stats, jnp.where(place & 2 == 0, ahead, back)]), 2)
    with jax.named_scope("far"):
        log, mixed = call(
            far_kernel,
            [like(tok, LANES, dtype=F32), like(*rows)],
            0,
            [],
            [vmem(*rows, dtype=F32)],
            smem=[where],
            vmem=[far, q, wk, wv, log, mixed],
            flops=100_000_000,
        )
    with jax.named_scope("halo"):
        y2, log = lax.optimization_barrier((y2, log))
        sides = jnp.stack([stats, jnp.where(place & 1 == 0, ahead, back)])
        core4 = swap(jnp.concatenate([sides, y2]), 1)
    with jax.named_scope("grad"):
        square, raw, wv = call(
            grad_kernel,
            [like(parts, LANES, dtype=F32), like(*rows, dtype=F32), like(*square_w)],
            0,
            [w_value],
            [vmem(3 * GROUP, blocks, packed), vmem(*rows), sems(10)],
            smem=[where],
            loose=[back, ahead, y2, core4, stats],
            vmem=[a, v, qk],
            flops=100_000_000,
        )
        two, square = lax.optimization_barrier((two, square))
        two_over = swap(two, 1)
        squares = lax.all_to_all(square, ("dp", "seq"), 0, 0)
    with jax.named_scope("rest"):
        (attn,) = call(
            rest_kernel,
            [like(*rows)],
            0,
            [w_key, mixed],
            [
                vmem(*square_w), vmem(*rows), vmem(3 * tok, width), vmem(3 * tok, width),
                vmem(*rows, dtype=F32), sems(2),
            ],
            smem=[where],
            loose=[square],
            vmem=[two, two_over, over, q, log, wv],
            flops=8_000_000_000,
        )
    with jax.named_scope("clip"):
        squares, attn = lax.optimization_barrier((squares, attn))
        entries = float(parts * tok * width)
        (grad,) = call(
            lambda *refs: scale_kernel(entries, *refs),
            [like(*rows, dtype=F32)],
            1,
            [],
            [vmem(*rows, dtype=F32), sems(4)],
            vmem=[squares, raw],
        )
    return attn[None], grad[None]


def solution(mesh):
    in_specs = (
        P("dp", "seq", None),
        P("dp", "seq", None),
        P("dp", "seq"),
        P("dp", "seq"),
        P("dp", "seq", None),
        P(),
        P(),
        P(),
        P(),
    )
    out_specs = (P("dp", "seq", None), P("dp", "seq", None))
    return jax.shard_map(
        on_device, mesh=mesh, in_specs=in_specs, out_specs=out_specs, check_vma=False
    )
```

```python
import math

import jax
import jax.numpy as jnp
from jax import lax
from jax.experimental import pallas as pl
from jax.experimental.pallas import tpu as pltpu
from jax.sharding import PartitionSpec as P

HEADS = 12
HEAD_DIM = 64
BLOCK = 16
WINDOW = 1024
LEVELS = 16
EPS = 1e-06
CLIP = 0.25
LANES = 128
NEVER = -1e30
SCALARS = 48
GROUP = 4
F32 = jnp.float32
BF16 = jnp.bfloat16
VMEM_LIMIT = 32 * 1024 * 1024
SCALE = 1.0 / math.sqrt(HEAD_DIM)


def iota(shape, dim):
    return lax.broadcasted_iota(jnp.int32, shape, dim)


def dot(a, b, precision=None):
    return jnp.dot(a, b, preferred_element_type=F32, precision=precision)


def dot_t(a, b, precision=None):
    return lax.dot_general(
        a, b, (((1,), (1,)), ((), ())), preferred_element_type=F32, precision=precision
    )


def token_mask_col(bits_row, tok):
    blocks = bits_row.shape[1]
    row, lane = iota((tok, blocks), 0), iota((tok, blocks), 1)
    bit = jnp.right_shift(jnp.broadcast_to(bits_row, (tok, blocks)), row % BLOCK) & 1
    return jnp.sum(jnp.where(row // BLOCK == lane, bit, 0).astype(F32), axis=1, keepdims=True)


def token_mask_row(bits_row, tok):
    blocks = bits_row.shape[1]
    diag = iota((blocks, blocks), 0) == iota((blocks, blocks), 1)
    col = jnp.sum(
        jnp.where(diag, jnp.broadcast_to(bits_row, (blocks, blocks)), 0).astype(F32),
        axis=1,
        keepdims=True,
    ).astype(jnp.int32)
    row, lane = iota((blocks, tok), 0), iota((blocks, tok), 1)
    bit = jnp.right_shift(jnp.broadcast_to(col, (blocks, tok)), lane % BLOCK) & 1
    return jnp.sum(jnp.where(lane // BLOCK == row, bit, 0).astype(F32), axis=0, keepdims=True)


def start_all(copies):
    for copy in copies:
        copy.start()
    return copies


def columns(at, count):
    return slice(at * count, (at + 1) * count)


def both_heads(pair):
    low = iota(pair.shape, 1) < HEAD_DIM
    wide = pair.astype(F32)
    return jnp.concatenate([jnp.where(low, wide, 0.0), jnp.where(low, 0.0, wide)], axis=0).astype(BF16)


def head_spread(width):
    return iota((LANES, width), 1) // HEAD_DIM == iota((LANES, width), 0)


def local_kernel(
    clean_hbm, wk_hbm, wv_hbm, wq_hbm, cot_hbm, me_hbm, bits_hbm, lev_hbm, imp_hbm,
    stats_ref, a_ref, qk_ref, km_ref, vm_ref, flags_ref, q_ref, k_ref, v_ref,
    clean_ref, wk_ref, wv_ref, wq_ref, cot_ref, me_ref, bits_ref, lev_ref, imp_ref, in_sems,
):
    sources = (clean_hbm, me_hbm, wk_hbm, wv_hbm, wq_hbm, bits_hbm, lev_hbm, imp_hbm, cot_hbm)
    targets = (clean_ref, me_ref, wk_ref, wv_ref, wq_ref, bits_ref, lev_ref, imp_ref, cot_ref)
    copies = start_all(
        [
            pltpu.make_async_copy(src, dst, in_sems.at[i])
            for i, (src, dst) in enumerate(zip(sources, targets))
        ]
    )
    tok, width = clean_ref.shape
    blocks = tok // BLOCK
    head_of = head_spread(width)
    spread = jnp.where(head_of, 1.0, 0.0).astype(BF16)
    copies[0].wait()
    copies[1].wait()
    mask_rows = jnp.broadcast_to(me_ref[...].reshape(1, width), (BLOCK, width))
    rows = jnp.concatenate([clean_ref[...], mask_rows], axis=0)
    copies[2].wait()
    keys = dot(rows, wk_ref[...]).astype(BF16)
    k_ref[...] = keys[:tok]
    km_ref[...] = keys[tok:]
    copies[3].wait()
    values = dot(rows, wv_ref[...]).astype(BF16)
    v_ref[...] = values[:tok]
    vm_ref[...] = values[tok:]
    copies[4].wait()
    queries = (dot(rows, wq_ref[...]).astype(BF16).astype(F32) * SCALE).astype(BF16)
    for copy in copies[5:]:
        copy.wait()
    bits = bits_ref[...]
    masked = token_mask_col(bits, tok)
    is_masked = masked > 0.5
    qm, vm = queries[tok : tok + 1], values[tok : tok + 1]
    q_ref[...] = jnp.where(is_masked, qm.astype(F32), queries[:tok].astype(F32)).astype(BF16)
    flags_ref[...] = jnp.broadcast_to(token_mask_row(bits, tok), flags_ref.shape)
    imp = imp_ref[...].astype(F32)
    weight = LEVELS / lev_ref[...].astype(F32) * (imp[0:1] / imp[1:2])
    row, lane = iota((tok, blocks), 0), iota((tok, blocks), 1)
    token_weight = masked * jnp.sum(
        jnp.where(row // BLOCK == lane, jnp.broadcast_to(weight, (tok, blocks)), 0.0),
        axis=1,
        keepdims=True,
    )
    grad = (cot_ref[...].astype(F32) * token_weight).astype(BF16)
    qm_heads = jnp.where(head_of, jnp.broadcast_to(qm.astype(F32), (LANES, width)), 0.0).astype(BF16)
    score = dot_t(keys, qm_heads)
    own, mask_score = score[:tok], score[tok : tok + 1]
    a_ref[...] = own
    back = dot_t(qm_heads, wk_ref[...])[:BLOCK]
    high = back.astype(BF16)
    low = (back - high.astype(F32)).astype(BF16)
    qk_ref[...] = jnp.zeros(qk_ref.shape, BF16)
    qk_ref[0:BLOCK] = high
    qk_ref[BLOCK : 2 * BLOCK] = high
    qk_ref[2 * BLOCK : 3 * BLOCK] = low

    def block_sums(scores, vals):
        by_block = scores.reshape(blocks, BLOCK, LANES)
        top = jnp.max(by_block, axis=1)
        expo = jnp.exp(by_block - top[:, None, :])
        total = jnp.sum(expo, axis=1)
        share = expo * (1.0 / total)[:, None, :]
        wide = dot(share.reshape(tok, LANES).astype(BF16), spread)
        mixed = jnp.sum((wide * vals).reshape(blocks, BLOCK, width), axis=1)
        return top + jnp.log(total), mixed

    value_f = values[:tok].astype(F32)
    top, mixed = block_sums(own, value_f)
    top_n, mixed_n = block_sums(
        jnp.where(is_masked, mask_score, own), jnp.where(is_masked, vm.astype(F32), value_f)
    )
    grad_sum = jnp.sum(grad.astype(F32).reshape(blocks, BLOCK, width), axis=1)
    product = grad_sum * mixed_n
    high = product.astype(BF16)
    low = (product - high.astype(F32)).astype(BF16)
    grad_mix = dot_t(high, spread) + dot_t(low, spread)
    in_heads = iota((blocks, LANES), 1) < HEADS
    packed = jnp.where(in_heads, top, 0.0)
    for place, part in enumerate((top_n, grad_mix)):
        packed = packed + pltpu.roll(jnp.where(in_heads, part, 0.0), 16 * (place + 1), 1)
    high = packed.astype(BF16).astype(F32)
    rest = packed - high
    mid = rest.astype(BF16).astype(F32)
    low = rest - mid
    stats_ref[:, 0:width] = grad_sum.astype(BF16)
    stats_ref[:, width : 2 * width] = mixed.astype(BF16)
    stats_ref[:, 2 * width : 2 * width + LANES] = (high + pltpu.roll(mid, SCALARS, 1)).astype(BF16)
    stats_ref[:, 2 * width + LANES :] = low.astype(BF16)


def grad_kernel(
    back_hbm, ahead_hbm, y_hbm, c_hbm, own_hbm, wv_hbm, a_ref, v_ref, qk_ref,
    square_ref, raw_ref, wv_ref,
    held, dvalues, in_sems,
):
    tok, width = v_ref.shape
    blocks = tok // BLOCK
    mine = lax.axis_index("seq")
    last = lax.axis_size("seq") * blocks
    at = mine % GROUP
    held[...] = jnp.zeros(held.shape, BF16)
    y_side = jnp.where(at & 2 == 0, 0, 2 * GROUP)
    c_side = jnp.where(at & 1 == 0, 0, 2 * GROUP)
    moves = (
        (back_hbm, held.at[at]),
        (own_hbm, held.at[GROUP + at]),
        (ahead_hbm, held.at[2 * GROUP + at]),
        (y_hbm.at[0], held.at[GROUP + (at ^ 2)]),
        (y_hbm.at[1], held.at[y_side + (at ^ 2)]),
        (c_hbm.at[0], held.at[GROUP + (at ^ 1)]),
        (c_hbm.at[1], held.at[c_side + (at ^ 1)]),
        (c_hbm.at[2], held.at[GROUP + (at ^ 3)]),
        (c_hbm.at[3], held.at[y_side + (at ^ 3)]),
        (wv_hbm, wv_ref),
    )
    copies = start_all(
        [pltpu.make_async_copy(src, dst, in_sems.at[i]) for i, (src, dst) in enumerate(moves)]
    )
    near = GROUP * blocks
    count_b = 2 * near
    count_u = 3 * near
    pad_u = 4 * near
    first_block = (mine - at - GROUP) * blocks
    u_at = iota((count_u, count_b), 0)
    b_at = iota((count_u, count_b), 1) + near
    seen = (u_at < b_at) & (u_at >= b_at - near) & (u_at + first_block >= 0)
    bias = jnp.where(seen, 0.0, -jnp.inf)
    for copy in copies[:9]:
        copy.wait()
    grads = held[GROUP:, :, 0:width].reshape(count_b, width)
    mixed = held[:, :, width : 2 * width].reshape(count_u, width)
    scalars = held[:, :, 2 * width : 2 * width + LANES].astype(F32).reshape(count_u, LANES)
    scalars = scalars + pltpu.roll(scalars, LANES - SCALARS, 1)
    scalars = scalars + held[:, :, 2 * width + LANES :].astype(F32).reshape(count_u, LANES)
    padded = jnp.concatenate(
        [scalars[near:], jnp.zeros((pad_u - count_b, LANES), F32)], axis=0
    )
    flipped = padded.T[:, :count_b]
    logs, deltas = [], []
    for pair_at in range(HEADS // 2):
        pair = columns(pair_at, LANES)
        products = dot_t(both_heads(mixed[:, pair]), grads[:, pair])
        for half in range(2):
            h = 2 * pair_at + half
            top = scalars[:, h : h + 1] + bias
            top_n = flipped[16 + h : 17 + h]
            peak = jnp.maximum(jnp.max(top, axis=0, keepdims=True), top_n)
            expo = jnp.exp(top - peak)
            expo_n = jnp.exp(top_n - peak)
            den = jnp.sum(expo, axis=0, keepdims=True) + expo_n
            delta = jnp.sum(expo * products[columns(half, count_u)], axis=0, keepdims=True)
            delta = (delta + expo_n * flipped[32 + h : 33 + h]) / den
            logs.append(peak + jnp.log(den))
            deltas.append(delta)
    own_at = near + at * blocks + iota((tok, count_b), 0) // BLOCK
    b_at = iota((tok, count_b), 1) + near
    seen = (own_at < b_at) & (own_at >= b_at - near) & (b_at + first_block < last)
    bias = jnp.where(seen, 0.0, -jnp.inf)
    lane_u = iota((tok, LANES), 1)
    terms = []
    scores = a_ref[...]
    for pair_at in range(HEADS // 2):
        pair = columns(pair_at, LANES)
        grad_pair = grads[:, pair]
        dprobs = dot_t(both_heads(v_ref[:, pair]), grad_pair)
        probs = []
        for half in range(2):
            h = 2 * pair_at + half
            prob = jnp.exp(scores[:, h : h + 1] - logs[h] + bias)
            term = prob * (dprobs[columns(half, tok)] - deltas[h])
            terms.append(term.astype(BF16))
            probs.append(prob.astype(BF16))
        parts = dot(jnp.concatenate(probs, axis=0), grad_pair)
        dvalues[:, pair] = jnp.where(lane_u < HEAD_DIM, parts[:tok], parts[tok:]).astype(BF16)
    to_head = iota((HEADS * count_b, LANES), 0) // count_b == iota((HEADS * count_b, LANES), 1)
    sigma = dot(jnp.concatenate(terms, axis=1), jnp.where(to_head, 1.0, 0.0).astype(BF16))
    high = sigma.astype(BF16).astype(F32)
    low = (sigma - high).astype(BF16).astype(F32)
    split = (high + pltpu.roll(low, 16, 1) + pltpu.roll(high, 32, 1)).astype(BF16)
    copies[9].wait()
    raw = dot_t(dvalues[...], wv_ref[...]) + dot(split, qk_ref[...])
    raw_ref[...] = raw
    total = jnp.sum(raw * raw, axis=0, keepdims=True)
    total = jnp.sum(total, axis=1, keepdims=True)
    square_ref[...] = jnp.broadcast_to(total, square_ref.shape)


def own_kernel(
    wk_hbm, wv_hbm, q_ref, k_ref, v_ref, km_ref, vm_ref, flags_ref,
    log_ref, mixed_ref, wk_ref, wv_ref,
    sems,
):
    tok, width = q_ref.shape
    pairs = HEADS // 2
    copies = start_all(
        [
            pltpu.make_async_copy(src, dst, sems.at[i])
            for i, (src, dst) in enumerate(((wk_hbm, wk_ref), (wv_hbm, wv_ref)))
        ]
    )
    row_b, col_b = iota((tok, tok), 0) // BLOCK, iota((tok, tok), 1) // BLOCK
    masked = flags_ref[0:1]
    own_bias = jnp.where((col_b < row_b) | ((col_b == row_b) & (masked < 0.5)), 0.0, -jnp.inf)
    count = jnp.sum(jnp.where(row_b == col_b, masked, 0.0), axis=1, keepdims=True)
    mask_bias = jnp.where(iota((tok, LANES), 1).astype(F32) < count, 0.0, -jnp.inf)
    bias = jnp.concatenate([own_bias, mask_bias], axis=1)
    bias = jnp.concatenate([bias, bias], axis=0)
    lane = iota((tok, LANES), 1)
    logs = jnp.zeros((tok, LANES), F32)
    for pair_at in range(pairs):
        pair = columns(pair_at, LANES)
        k_mask = jnp.broadcast_to(km_ref[0:1, pair], (LANES, LANES))
        v_mask = jnp.broadcast_to(vm_ref[0:1, pair], (LANES, LANES))
        keys = jnp.concatenate([k_ref[:, pair], k_mask], axis=0)
        vals = jnp.concatenate([v_ref[:, pair], v_mask], axis=0)
        score = dot_t(both_heads(q_ref[:, pair]), keys) + bias
        peak = jnp.max(score, axis=1, keepdims=True)
        expo = jnp.exp(score - peak)
        den = jnp.sum(expo, axis=1, keepdims=True)
        mixed = dot(expo.astype(BF16), vals) / den
        log = peak + jnp.log(den)
        logs = jnp.where(lane == 2 * pair_at, log[:tok], logs)
        logs = jnp.where(lane == 2 * pair_at + 1, log[tok:], logs)
        mixed_ref[:, pair] = jnp.where(lane < HEAD_DIM, mixed[:tok], mixed[tok:]).astype(BF16)
    log_ref[...] = logs
    for copy in copies:
        copy.wait()


def attend_pair(q_pair, keys, vals, biases):
    tok = q_pair.shape[0]
    score = dot_t(both_heads(q_pair), keys)
    pieces = [score[:, columns(place, tok)] + bias for place, bias in enumerate(biases)]
    peak = pieces[0]
    for piece in pieces[1:]:
        peak = jnp.maximum(peak, piece)
    peak = jnp.max(peak, axis=1, keepdims=True)
    expo = jnp.concatenate([jnp.exp(piece - peak).astype(BF16) for piece in pieces], axis=1)
    mixed = dot(expo, jnp.concatenate([vals, jnp.ones(vals.shape, BF16)], axis=1))
    mixed, den = mixed[:, :LANES] / mixed[:, LANES:], mixed[:, LANES:]
    low = iota((tok, LANES), 1) < HEAD_DIM
    return jnp.where(low, mixed[:tok], mixed[tok:]), peak + jnp.log(den)


def keep_logs(logs, pair_at, log):
    tok = logs.shape[0]
    lane = iota(logs.shape, 1)
    logs = jnp.where(lane == 2 * pair_at, log[:tok], logs)
    return jnp.where(lane == 2 * pair_at + 1, log[tok:], logs)


def blend(logs, total, old_logs, old_mixed):
    share = 1.0 / (1.0 + jnp.exp(logs - old_logs))
    high = share.astype(BF16)
    low = (share - high.astype(F32)).astype(BF16)
    spread = jnp.where(head_spread(total.shape[1]), 1.0, 0.0).astype(BF16)
    share = dot(high, spread) + dot(low, spread)
    return (total + share * (old_mixed.astype(F32) - total)).astype(BF16)


def far_kernel(
    far_ref, q_ref, wk_ref, wv_ref, old_log_ref, old_mixed_ref,
    log_ref, mixed_ref,
    total_ref,
):
    tok, width = q_ref.shape
    row_b, col_b = iota((tok, tok), 0) // BLOCK, iota((tok, tok), 1) // BLOCK
    bias = jnp.where((col_b >= row_b) & (lax.axis_index("seq") >= GROUP), 0.0, NEVER)
    bias = jnp.concatenate([bias, bias], axis=0)
    keys = dot(far_ref[...], wk_ref[...]).astype(BF16)
    vals = dot(far_ref[...], wv_ref[...]).astype(BF16)
    logs = jnp.zeros((tok, LANES), F32)
    for pair_at in range(HEADS // 2):
        pair = columns(pair_at, LANES)
        mixed, log = attend_pair(q_ref[:, pair], keys[:, pair], vals[:, pair], [bias])
        total_ref[:, pair] = mixed
        logs = keep_logs(logs, pair_at, log)
    old = old_log_ref[...]
    mixed_ref[...] = blend(logs, total_ref[...], old, old_mixed_ref[...])
    top = jnp.maximum(logs, old)
    log_ref[...] = top + jnp.log(jnp.exp(logs - top) + jnp.exp(old - top))


def rest_kernel(
    after_hbm, wk_hbm, mixed_hbm,
    two_ref, two_over_ref, over_ref, q_ref, log_ref, wv_ref,
    out_ref,
    wk_ref, mixed_ref, keys, vals, total_ref, in_sems,
):
    tok, width = q_ref.shape
    rows = (two_ref, two_over_ref, over_ref)
    shards = len(rows)
    mine = lax.axis_index("seq")
    part = 2 * LANES
    parts = width // part
    key_copy = pltpu.make_async_copy(wk_hbm, wk_ref, in_sems.at[0])
    key_copy.start()
    mixed_copy = pltpu.make_async_copy(mixed_hbm, mixed_ref, in_sems.at[1])
    mixed_copy.start()
    over = jnp.where(mine & 1 == 0, 1, 3)
    biases = [jnp.where(mine >= back, 0.0, NEVER) for back in (2, over, 4 - over)]

    def project(weight, kept):
        for at in range(parts):
            cols = columns(at, part)
            for place in range(shards):
                kept[columns(place, tok), cols] = dot(rows[place][...], weight[:, cols]).astype(BF16)

    project(wv_ref, vals)
    key_copy.wait()
    project(wk_ref, keys)
    logs = jnp.zeros((tok, LANES), F32)
    for pair_at in range(HEADS // 2):
        pair = columns(pair_at, LANES)
        mixed, log = attend_pair(q_ref[:, pair], keys[:, pair], vals[:, pair], biases)
        total_ref[:, pair] = mixed
        logs = keep_logs(logs, pair_at, log)
    mixed_copy.wait()
    out_ref[...] = blend(logs, total_ref[...], log_ref[...], mixed_ref[...])


def scale_kernel(entries, square_ref, raw_ref, out_hbm, out_ref, sems):
    tok = raw_ref.shape[0]
    pieces = 4
    total = jnp.sum(square_ref[:, 0:1], axis=0, keepdims=True)
    rms = jnp.sqrt(total / entries + EPS)
    factor = jnp.minimum(1.0, CLIP / rms)
    outs = []
    for at in range(pieces):
        span = columns(at, tok // pieces)
        out_ref[span] = raw_ref[span] * factor
        outs.append(pltpu.make_async_copy(out_ref.at[span], out_hbm.at[span], sems.at[at]))
        outs[-1].start()
    for copy in outs:
        copy.wait()


def call(kernel, out_shape, hbm_out, args, scratch, vmem=(), loose=(), flops=0):
    args = [pltpu.with_memory_space_constraint(array, pltpu.HBM) for array in args]
    args = [*loose, *args, *vmem]
    kinds = [pl.ANY] * (len(args) - len(vmem)) + [pltpu.VMEM] * len(vmem)
    out_kinds = [pltpu.VMEM] * (len(out_shape) - hbm_out) + [pl.ANY] * hbm_out
    return pl.pallas_call(
        kernel,
        out_shape=out_shape,
        in_specs=[pl.BlockSpec(memory_space=kind) for kind in kinds],
        out_specs=[pl.BlockSpec(memory_space=kind) for kind in out_kinds],
        scratch_shapes=scratch,
        compiler_params=pltpu.CompilerParams(vmem_limit_bytes=VMEM_LIMIT),
        cost_estimate=pl.CostEstimate(flops=flops, bytes_accessed=1 << 10, transcendentals=0),
    )(*args)


def shift(rows, distance):
    devices = range(lax.axis_size("seq"))
    return lax.ppermute(rows, "seq", [(i, i + distance) for i in devices if i + distance in devices])


def swap(rows, bit):
    return lax.ppermute(rows, "seq", [(i, i ^ bit) for i in range(lax.axis_size("seq"))])


def on_device(clean, out_cot, mask_bits, levels, importance, w_query, w_key, w_value, mask_embed):
    clean_rows = clean[0]
    tok, width = clean_rows.shape
    blocks = tok // BLOCK
    place = lax.axis_index("seq")
    count = lax.axis_size("seq")
    parts = lax.axis_size("dp") * count
    rows = (tok, width)
    square_w = (width, width)
    packed = 2 * width + 2 * LANES

    def like(*dims, dtype=BF16):
        return jax.ShapeDtypeStruct(dims, dtype)

    def vmem(*dims, dtype=BF16):
        return pltpu.VMEM(dims, dtype)

    def sems(count):
        return pltpu.SemaphoreType.DMA((count,))

    with jax.named_scope("halo"):
        far = shift(clean_rows, GROUP)
    with jax.named_scope("local"):
        ratio = importance[0].T
        stats, a, qk, km, vm, flags, q, k, v = call(
            local_kernel,
            [
                like(blocks, packed), like(tok, LANES, dtype=F32), like(LANES, width),
                like(BLOCK, width), like(BLOCK, width), like(8, tok, dtype=F32),
                like(*rows), like(*rows), like(*rows),
            ],
            0,
            [clean_rows, w_key, w_value, w_query, out_cot[0], mask_embed, mask_bits, levels, ratio],
            [
                vmem(*rows), vmem(*square_w), vmem(*square_w), vmem(*square_w), vmem(*rows),
                vmem(width), vmem(1, blocks, dtype=jnp.int32), vmem(1, blocks, dtype=jnp.int32),
                vmem(2, blocks, dtype=jnp.int32), sems(9),
            ],
            flops=1_000_000_000,
        )
    with jax.named_scope("halo"):
        back, ahead = shift(stats, GROUP), shift(stats, -GROUP)
        other = jnp.where(place & 2 == 0, clean_rows, far)
        q, other = lax.optimization_barrier((q, other))
        two = swap(other, 2)
    with jax.named_scope("own"):
        log, mixed, wk, wv = call(
            own_kernel,
            [like(tok, LANES, dtype=F32), like(*rows), like(*square_w), like(*square_w)],
            0,
            [w_key, w_value],
            [sems(2)],
            vmem=[q, k, v, km, vm, flags],
            flops=1_000_000_000,
        )
    with jax.named_scope("halo"):
        back, ahead, log = lax.optimization_barrier((back, ahead, log))
        over = swap(jnp.where(place & 1 == 0, clean_rows, far), 1)
        y2 = swap(jnp.stack([stats, jnp.where(place & 2 == 0, ahead, back)]), 2)
    with jax.named_scope("far"):
        log, mixed = call(
            far_kernel,
            [like(tok, LANES, dtype=F32), like(*rows)],
            0,
            [],
            [vmem(*rows, dtype=F32)],
            vmem=[far, q, wk, wv, log, mixed],
            flops=100_000_000,
        )
    with jax.named_scope("halo"):
        y2, log = lax.optimization_barrier((y2, log))
        sides = jnp.stack([stats, jnp.where(place & 1 == 0, ahead, back)])
        core4 = swap(jnp.concatenate([sides, y2]), 1)
    with jax.named_scope("grad"):
        square, raw, wv = call(
            grad_kernel,
            [like(parts, LANES, dtype=F32), like(*rows, dtype=F32), like(*square_w)],
            0,
            [w_value],
            [vmem(3 * GROUP, blocks, packed), vmem(*rows), sems(10)],
            loose=[back, ahead, y2, core4, stats],
            vmem=[a, v, qk],
            flops=100_000_000,
        )
        two, square = lax.optimization_barrier((two, square))
        two_over = swap(two, 1)
        squares = lax.all_to_all(square, ("dp", "seq"), 0, 0)
    with jax.named_scope("rest"):
        (attn,) = call(
            rest_kernel,
            [like(*rows)],
            0,
            [w_key, mixed],
            [
                vmem(*square_w), vmem(*rows), vmem(3 * tok, width), vmem(3 * tok, width),
                vmem(*rows, dtype=F32), sems(2),
            ],
            loose=[square],
            vmem=[two, two_over, over, q, log, wv],
            flops=8_000_000_000,
        )
    with jax.named_scope("clip"):
        squares, attn = lax.optimization_barrier((squares, attn))
        entries = float(parts * tok * width)
        (grad,) = call(
            lambda *refs: scale_kernel(entries, *refs),
            [like(*rows, dtype=F32)],
            1,
            [],
            [vmem(*rows, dtype=F32), sems(4)],
            vmem=[squares, raw],
        )
    return attn[None], grad[None]


def solution(mesh):
    in_specs = (
        P("dp", "seq", None),
        P("dp", "seq", None),
        P("dp", "seq"),
        P("dp", "seq"),
        P("dp", "seq", None),
        P(),
        P(),
        P(),
        P(),
    )
    out_specs = (P("dp", "seq", None), P("dp", "seq", None))
    return jax.shard_map(
        on_device, mesh=mesh, in_specs=in_specs, out_specs=out_specs, check_vma=False
    )
```
